32 devices in a mesh: ctx: 8 (over z, x), tp: 4 (over y, core).
Axes of the slice: x: 2, y: 2, z: 4, core: 2. Of those that a mesh axis runs over, the one named last changes fastest.
Arguments:
- x_in: bfloat16 [4096, 4096], P('ctx', 'tp'), may hold values from -6 to 6
- bc_in: bfloat16 [4096, 256], P('ctx'), may hold values from -6 to 6
- z_in: bfloat16 [4096, 4096], P('ctx', 'tp'), may hold values from -6 to 6
- codes: int32 [4096, 32], P('ctx', 'tp'), may hold values from 0 to 63
- head_rate: float32 [32], P('tp'), may hold values from 0.25 to 1
- conv_x: float32 [4, 4096], P(None, 'tp'), may hold values from -3 to 3
- conv_bc: float32 [4, 256], replicated, may hold values from -3 to 3
- bias_x: float32 [4096], P('tp'), may hold values from -2 to 2
- bias_bc: float32 [256], replicated, may hold values from -2 to 2
- skip: float32 [32], P('tp'), may hold values from 0.5 to 1.5
- norm_gain: float32 [4096], P('tp'), may hold values from 0.5 to 1.5
- w_out: bfloat16 [4096, 8192], P('tp'), may hold values from -0.125 to 0.125
Outputs:
- mixed: bfloat16 [4096, 8192], P('ctx', 'tp')
The draws below stay inside these ranges and needn't reach their ends.
All inputs are finite; a program needn't handle non-finite values.
Results may differ from the reference program's by a relative error of at most 0.019.
Values may be sent and summed in bfloat16 or wider, within the bound.
A program may use at most 128 MiB of HBM per device.

```python
import math
import jax
import jax.numpy as jnp
from jax import lax

DM = 8192
P_SIZE = 128
N = 128
TOK_DEV = 512
HEADS = 32
SEQ = 4096
N_TP = 4


def draw_codes(key, part):
    key_cap, key_raw = jax.random.split(jax.random.fold_in(key, 7))
    shard_count = SEQ // TOK_DEV
    caps = jax.random.randint(key_cap, (shard_count, 1, HEADS), 0, 64)
    raw = jax.random.randint(key_raw, (shard_count, TOK_DEV, HEADS), 0, 1048576)
    values = (raw % (caps + 1)).reshape(SEQ, HEADS)
    values = values.at[0].set(63)
    values = values.at[1].set(0)
    return values.astype(jnp.int32)


def strengthened(result, stream_key, source, target, blocks, factor):
    owner, partner = [(jnp.arange(result.shape[axis_at]) // (result.shape[axis_at] // blocks)).reshape([-1 if axis == axis_at else 1 for axis in range(result.ndim)]) for axis_at in (source, target)]
    chosen = jax.random.permutation(stream_key, blocks)[partner]
    strong = (owner == chosen) | (owner == (partner + blocks // 2) % blocks)
    return jnp.where(strong, factor * result, result)


def levels(rng, dims, cuts, low, top_value):
    gain = 1.0
    for position, shards_of in cuts:
        steps = jax.random.uniform(jax.random.fold_in(jax.random.fold_in(rng, 6), position), (shards_of,), jnp.float32, low / len(cuts), top_value / len(cuts))
        gain = gain * jnp.repeat(jnp.exp(steps), dims[position] // shards_of).reshape((-1,) + (1,) * (len(dims) - 1 - position))
    return gain


def normal_values(key, extent, deviation, reach, cuts=(), kind=jnp.bfloat16):
    entries = jax.random.normal(key, extent, jnp.float32) * deviation
    if len(cuts) > 0:
        entries = levels(key, extent, cuts, -0.22, 0.18) * entries
    return jnp.clip(entries, min=-reach, max=reach).astype(kind)


def heavy_noise(key, extent, width, bound, shards, heavy, kind=jnp.bfloat16):
    values = width * jax.random.normal(key, extent, jnp.float32)
    if shards:
        values = values * levels(key, extent, shards, -0.22, 0.18)
    return jnp.clip(strengthened(values, jax.random.fold_in(key, 3), *heavy), -bound, bound).astype(kind)


def setup_inputs(seed: int = 0) -> dict:
    arg_keys = jax.random.split(jax.random.key(seed), 13)
    x_in = normal_values(arg_keys[0], (SEQ, HEADS * P_SIZE), 1.0, 6.0, ((0, 8), (1, 4)))
    bc_in = normal_values(arg_keys[1], (SEQ, 2 * N), 1.0, 6.0, ((0, 8),))
    z_in = normal_values(arg_keys[2], (SEQ, HEADS * P_SIZE), 1.0, 6.0, ((0, 8), (1, 4)))
    codes = draw_codes(jax.random.fold_in(arg_keys[12], 71), 0)
    head_rate = jnp.clip(jnp.exp(math.log(1.0) - 1.3862944 * jax.random.uniform(arg_keys[4], (HEADS,), jnp.float32) ** levels(arg_keys[4], (HEADS,), ((0, 4),), -0.2, 0.2)), 0.25, 1.0)
    conv_x = normal_values(arg_keys[5], (4, HEADS * P_SIZE), 0.5, 3.0, ((1, 4),), jnp.float32)
    conv_bc = normal_values(arg_keys[6], (4, 2 * N), 0.5, 3.0, (), jnp.float32)
    bias_x = normal_values(arg_keys[7], (HEADS * P_SIZE,), 0.3, 2.0, ((0, 4),), jnp.float32)
    bias_bc = normal_values(arg_keys[8], (2 * N,), 0.3, 2.0, (), jnp.float32)
    skip = jnp.clip(0.5 + 1.0 * jax.random.uniform(arg_keys[9], (HEADS,), jnp.float32) ** levels(arg_keys[9], (HEADS,), ((0, 4),), -0.2, 0.2), 0.5, 1.5)
    norm_gain = jnp.clip(1.0 + 0.1 * jax.random.normal(arg_keys[10], (HEADS * P_SIZE,), jnp.float32), 0.5, 1.5)
    w_out = heavy_noise(arg_keys[11], (HEADS * P_SIZE, DM), (HEADS * P_SIZE) ** -0.5, 0.125, ((0, 4),), (0, 1, 4, 2.0))
    return dict(x_in=x_in, bc_in=bc_in, z_in=z_in, codes=codes, head_rate=head_rate, conv_x=conv_x, conv_bc=conv_bc, bias_x=bias_x, bias_bc=bias_bc, skip=skip, norm_gain=norm_gain, w_out=w_out)


def causal_conv(signal, weight, shift_bias):
    tok_count = signal.shape[0]
    padded = jnp.pad(signal.astype(jnp.float32), ((3, 0), (0, 0)))
    total = shift_bias[None, :]
    for k in range(4):
        total = total + weight[k][None, :] * padded[k:k + tok_count]
    return jax.nn.silu(total).astype(jnp.bfloat16)

def reference(x_in, bc_in, z_in, codes, head_rate, conv_x, conv_bc, bias_x, bias_bc, skip, norm_gain, w_out):
    high = lax.Precision.HIGHEST
    wide = lax.Precision.HIGH
    xc = causal_conv(x_in, conv_x, bias_x).reshape(SEQ, HEADS, P_SIZE)
    bcc = causal_conv(bc_in, conv_bc, bias_bc)
    in_maps = bcc[:, :N]
    out_maps = bcc[:, N:]
    log_decay = -12.288 / SEQ * head_rate[None, :] * codes.astype(jnp.float32) / 63.0
    cum = jnp.cumsum(log_decay, axis=0)
    block_len = math.gcd(TOK_DEV, 128)
    block_count = SEQ // block_len
    x_blocks = xc.reshape(block_count, block_len, HEADS, P_SIZE)
    in_blocks = in_maps.reshape(block_count, block_len, N)
    out_blocks = out_maps.reshape(block_count, block_len, N)
    cum_blocks = cum.reshape(block_count, block_len, HEADS)
    starts = jnp.concatenate([jnp.zeros((1, HEADS), jnp.float32), cum_blocks[:-1, -1]], axis=0)
    causal = jnp.tril(jnp.ones((block_len, block_len), dtype=bool))

    def advance(running_state, inputs):
        x_block, in_block, out_block, cum_block, block_start = inputs
        scores = jnp.dot(out_block, in_block.T, preferred_element_type=jnp.float32)
        log_gap = cum_block[:, None, :] - cum_block[None, :, :]
        mask3 = causal[:, :, None]
        weights = jnp.where(mask3, jnp.exp(jnp.where(mask3, log_gap, 0.0)), 0.0) * scores[:, :, None]
        weights = weights.astype(jnp.bfloat16)
        inside = jnp.einsum('tsh,shp->thp', weights, x_block, preferred_element_type=jnp.float32)
        carried = jnp.einsum('tn,hnp->thp', out_block.astype(jnp.float32), running_state, precision=wide)
        carried = carried * jnp.exp(cum_block - block_start[None, :])[:, :, None]
        block_end = cum_block[-1]
        factors = jnp.exp(block_end[None, :] - cum_block)
        sent = (x_block.astype(jnp.float32) * factors[:, :, None]).astype(jnp.bfloat16)
        added = jnp.einsum('sn,shp->hnp', in_block, sent, preferred_element_type=jnp.float32)
        next_state = jnp.exp(block_end - block_start)[:, None, None] * running_state + added
        return (next_state, inside + carried)
    _, outputs = lax.scan(advance, jnp.zeros((HEADS, N, P_SIZE), jnp.float32), (x_blocks, in_blocks, out_blocks, cum_blocks, starts))
    scanned = outputs.reshape(SEQ, HEADS, P_SIZE)
    ssd_scale = 1.0 / math.sqrt(N * SEQ)
    ssd = scanned * ssd_scale + skip[None, :, None] * xc.astype(jnp.float32)
    gated_out = ssd * jax.nn.silu(z_in.astype(jnp.float32).reshape(SEQ, HEADS, P_SIZE))
    mean_square = lax.optimization_barrier(jnp.mean(gated_out * gated_out, axis=-1, keepdims=True))
    normed = gated_out * lax.rsqrt(mean_square + 1e-05) * norm_gain.reshape(HEADS, P_SIZE)[None]
    normed = normed.astype(jnp.bfloat16).reshape(SEQ, HEADS * P_SIZE)
    group_width = HEADS * P_SIZE // N_TP
    normed_groups = jnp.transpose(normed.reshape(SEQ, N_TP, group_width), (1, 0, 2))
    weight_groups = w_out.reshape(N_TP, group_width, DM)

    def add_group(total, pair):
        group_rows, group_weight = pair
        partial_value = jnp.dot(group_rows.astype(jnp.float32), group_weight.astype(jnp.float32), precision=high)
        partial_value = lax.optimization_barrier(partial_value.astype(jnp.bfloat16)).astype(jnp.float32)
        return (total + partial_value, None)
    total, _ = lax.scan(add_group, jnp.zeros((SEQ, DM), jnp.float32), (normed_groups, weight_groups))
    return total.astype(jnp.bfloat16)
```

```python
import functools
import math

import jax
import jax.numpy as jnp
from jax import lax
from jax.experimental import pallas as pl
from jax.experimental.pallas import tpu as pltpu
from jax.sharding import PartitionSpec as P

MESH = pl.DeviceIdType.MESH
F32 = jnp.float32
BF16 = jnp.bfloat16
BLOCK = 128
GROUP = 256
RIM = 16


def silu(v):
    return v / (1.0 + jnp.exp(-v))


def conv(window, taps, bias):
    total = bias + taps[3:4] * window[RIM:]
    for k in range(3):
        total = total + taps[k : k + 1] * pltpu.roll(window, 3 - k, 0)[RIM:]
    return silu(total).astype(BF16)


def layer(
    n_ctx,
    n_tp,
    n_x,
    x_ref, bc_ref, z_ref, codes_ref, rate_ref, cx_ref, cbc_ref, bx_ref, bbc_ref, skip_ref, gain_ref, w_ref,
    out_ref,
    rim_x, rim_bc, tril, coded, coef, skips, ec, en, bcc, bt, xc, us, states, pz, pz_next, pin,
    g_all, h_all, own_n, sib_n, w_own, w_sib, y_send, y_recv, local,
    rim_send, rim_recv, wl_sem, ws_send, ws_recv, x_send, x_recv, z_send, z_recv, n_send, n_recv, ys_send, ys_recv,
):
    toks, width = x_ref.shape
    heads = skip_ref.shape[0]
    n_z = n_ctx // n_x
    n_y = n_tp // 2
    blocks = toks // BLOCK
    groups = width // GROUP
    owned = out_ref.shape[1]
    part = y_send.shape[3]
    parts = owned // part
    ctx = lax.axis_index("ctx")
    tp = lax.axis_index("tp")
    iz, ix = ctx // n_x, ctx % n_x
    iy, core = tp // 2, tp % 2
    sib = tp + 1 - 2 * core
    seq = toks * n_ctx
    n_state = bc_ref.shape[1] // 2

    barrier = pltpu.get_barrier_semaphore()

    def greet(c, t):
        pl.semaphore_signal(barrier, inc=1, device_id=(c, t), device_id_type=MESH)

    greet(ctx, sib)
    for r in range(1, n_y):
        greet(ctx, (iy + r) % n_y * 2 + core)
    for r in range(1, n_x):
        greet(iz * n_x + (ix + r) % n_x, tp)
    for near, far in ((ctx > 0, ctx - 1), (ctx < n_ctx - 1, ctx + 1), (iz > 0, ctx - n_x), (iz < n_z - 1, ctx + n_x)):
        pl.when(near)(functools.partial(greet, far, tp))
    count = n_y + n_x - 1
    for near in (ctx > 0, ctx < n_ctx - 1, iz > 0, iz < n_z - 1):
        count = count + jnp.where(near, 1, 0)
    pl.semaphore_wait(barrier, count)

    def remote(src, dst, send, recv, c, t):
        return pltpu.make_async_remote_copy(
            src_ref=src, dst_ref=dst, send_sem=send, recv_sem=recv, device_id=(c, t), device_id_type=MESH
        )

    rims = [
        remote(x_ref.at[pl.ds(toks - RIM, RIM)], rim_x, rim_send.at[0], rim_recv.at[0], ctx + 1, tp),
        remote(bc_ref.at[pl.ds(toks - RIM, RIM)], rim_bc, rim_send.at[1], rim_recv.at[1], ctx + 1, tp),
    ]

    @pl.when(ctx < n_ctx - 1)
    def _():
        for copy in rims:
            copy.start()

    order = list(range(1, n_y)) + [0]
    w_loads, w_swaps = {}, {}
    for r in order:
        chip = (iy + r) % n_y
        mine = pl.ds(pl.multiple_of((chip * 2 + core) * owned, GROUP), owned)
        theirs = pl.ds(pl.multiple_of((chip * 2 + 1 - core) * owned, GROUP), owned)
        w_loads[r] = pltpu.make_async_copy(w_ref.at[:, mine], w_own.at[r], wl_sem.at[r])
        w_swaps[r] = remote(w_ref.at[:, theirs], w_sib.at[r], ws_send.at[r], ws_recv.at[r], ctx, sib)
        w_loads[r].start()
        w_swaps[r].start()

    row_id = lax.broadcasted_iota(jnp.int32, (toks, toks), 0)
    col_id = lax.broadcasted_iota(jnp.int32, (toks, toks), 1)
    tril[...] = jnp.where(row_id >= col_id, 1.0, 0.0).astype(BF16)
    codes = codes_ref[...].astype(F32)
    for h in range(heads):
        cols = slice(h * BLOCK, (h + 1) * BLOCK)
        coded[:, cols] = jnp.broadcast_to(codes[:, h : h + 1], (toks, BLOCK)).astype(BF16)
        coef[:, cols] = jnp.full((8, BLOCK), rate_ref[h] * (-12.288 / seq / 63.0), F32)
        skips[:, cols] = jnp.full((8, BLOCK), skip_ref[h], F32)

    def decays(j, _):
        cols = pl.ds(pl.multiple_of(j * GROUP, GROUP), GROUP)
        cum = jnp.dot(tril[...], coded[:, cols], preferred_element_type=F32) * coef[0:1, cols]
        ec[:, cols] = jnp.exp(cum)
        en[:, cols] = jnp.exp(-cum)
        return 0

    lax.fori_loop(0, groups, decays, 0)

    def conv_x(j, b):
        cols = pl.ds(pl.multiple_of(j * BLOCK, BLOCK), BLOCK)
        rows = pl.ds(b * BLOCK, BLOCK)
        if b == 0:
            window = jnp.concatenate([rim_x[:, cols], x_ref[rows, cols]], axis=0)
        else:
            window = x_ref[pl.ds(b * BLOCK - RIM, BLOCK + RIM), cols]
        value = conv(window.astype(F32), cx_ref[:, cols], bx_ref[:, cols])
        xc[rows, cols] = value
        us[rows, cols] = (value.astype(F32) * en[rows, cols]).astype(BF16)

    def conv_bc(b):
        rows = pl.ds(b * BLOCK, BLOCK)
        if b == 0:
            window = jnp.concatenate([rim_bc[...], bc_ref[rows, :]], axis=0)
        else:
            window = bc_ref[pl.ds(b * BLOCK - RIM, BLOCK + RIM), :]
        value = conv(window.astype(F32), cbc_ref[...], bbc_ref[...])
        bcc[rows, :] = value
        bt[:, b * BLOCK : (b + 1) * BLOCK] = value[:, :n_state].astype(F32).T.astype(BF16)

    def later_blocks(j, _):
        for b in range(1, blocks):
            conv_x(j, b)
        return 0

    def first_block(j, _):
        conv_x(j, 0)
        return 0

    for b in range(1, blocks):
        conv_bc(b)
    lax.fori_loop(0, width // BLOCK, later_blocks, 0)

    @pl.when(ctx == 0)
    def _():
        rim_x[...] = jnp.zeros_like(rim_x)
        rim_bc[...] = jnp.zeros_like(rim_bc)

    @pl.when(ctx > 0)
    def _():
        for copy in rims:
            copy.wait_recv()

    conv_bc(0)
    lax.fori_loop(0, width // BLOCK, first_block, 0)

    x_copies = {}
    for g in range(groups):
        cols = slice(g * GROUP, (g + 1) * GROUP)
        total = ec[toks - 1 : toks, cols]
        state = jnp.dot(bt[...], us[:, cols], preferred_element_type=F32)
        states[n_x - 1, :n_state, cols] = (state * total).astype(BF16)
        high = total.astype(BF16).astype(F32)
        pick = lax.broadcasted_iota(jnp.int32, (RIM, GROUP), 0) < 8
        states[n_x - 1, n_state:, cols] = jnp.where(pick, high, total - high).astype(BF16)
        for r in range(1, n_x):
            x_copies[r, g] = remote(
                states.at[n_x - 1, :, pl.ds(g * GROUP, GROUP)],
                states.at[r - 1, :, pl.ds(g * GROUP, GROUP)],
                x_send.at[r - 1, g], x_recv.at[r - 1, g],
                iz * n_x + (ix + r) % n_x, tp,
            )
            x_copies[r, g].start()

    scale = 1.0 / math.sqrt(n_state * seq)
    for b in range(blocks):
        rows = slice(b * BLOCK, (b + 1) * BLOCK)
        upto = (b + 1) * BLOCK
        scores = lax.dot_general(
            bcc[rows, n_state:], bcc[:upto, :n_state], (((1,), (1,)), ((), ())), preferred_element_type=F32
        )
        scores = (scores * tril[rows, :upto].astype(F32)).astype(BF16)

        def inside(j, _, rows=rows, upto=upto, scores=scores):
            cols = pl.ds(pl.multiple_of(j * GROUP, GROUP), GROUP)
            y = jnp.dot(scores, us[:upto, cols], preferred_element_type=F32)
            gate = silu(z_ref[rows, cols].astype(F32))
            decay = ec[rows, cols] * (scale * gate)
            g_all[rows, cols] = y * decay + skips[0:1, cols] * xc[rows, cols].astype(F32) * gate
            h_all[rows, cols] = decay
            return 0

        lax.fori_loop(0, groups, inside, 0)

    @pl.when(iz == 0)
    def _():
        pz[...] = jnp.zeros_like(pz)

    z_copies = []
    for g in range(groups):
        cols = slice(g * GROUP, (g + 1) * GROUP)
        span = pl.ds(g * GROUP, GROUP)
        copy = remote(pz_next.at[:, span], pz.at[:, span], z_send.at[g], z_recv.at[g], ctx + n_x, tp)
        z_copies.append(copy)
        for r in range(1, n_x):
            x_copies[r, g].wait_recv()
        pl.when(iz > 0)(copy.wait_recv)
        before = pz[:, cols].astype(F32)
        arrived = before
        for k in range(n_x):
            slot = (ix - k - 1 + n_x) % n_x
            arrived = jnp.where(ix == k, before, arrived)
            factor = states[slot, n_state : n_state + 1, cols].astype(F32)
            factor = factor + states[slot, n_state + 8 : n_state + 9, cols].astype(F32)
            before = before * factor + states[slot, :n_state, cols].astype(F32)
        pz_next[:, cols] = before.astype(BF16)
        pl.when(iz < n_z - 1)(copy.start)
        pin[:, cols] = arrived.astype(BF16)

    n_copies = []
    for b in range(blocks):
        span = pl.ds(b * BLOCK, BLOCK)
        n_copies.append(remote(own_n.at[span], sib_n.at[span], n_send.at[b], n_recv.at[b], ctx, sib))

    def norm(b):
        rows = slice(b * BLOCK, (b + 1) * BLOCK)

        def pair(j, _):
            start = pl.multiple_of(j * GROUP, GROUP)
            cols = pl.ds(start, GROUP)
            carried = jnp.dot(bcc[rows, n_state:], pin[:, cols], preferred_element_type=F32)
            gated = g_all[rows, cols] + h_all[rows, cols] * carried
            for half in range(GROUP // BLOCK):
                piece = gated[:, half * BLOCK : (half + 1) * BLOCK]
                mean_square = jnp.mean(piece * piece, axis=-1, keepdims=True)
                cut = pl.ds(pl.multiple_of(start + half * BLOCK, BLOCK), BLOCK)
                own_n[rows, cut] = (piece * lax.rsqrt(mean_square + 1e-05) * gain_ref[:, cut]).astype(BF16)
            return 0

        lax.fori_loop(0, groups, pair, 0)
        n_copies[b].start()

    def project(b, r, first, tiles, store):
        rows = slice(b * BLOCK, (b + 1) * BLOCK)

        def tile(j, _):
            cols = pl.ds(pl.multiple_of(first + j * GROUP, GROUP), GROUP)
            value = jnp.dot(own_n[rows, :], w_own[r, :, cols], preferred_element_type=F32)
            value = value + jnp.dot(sib_n[rows, :], w_sib[r, :, cols], preferred_element_type=F32)
            store(rows, j, cols, value)
            return 0

        lax.fori_loop(0, tiles, tile, 0)

    y_copies = {}

    def send_block(b):
        n_copies[b].wait_recv()
        for r in range(1, n_y):
            if b == 0:
                w_loads[r].wait()
                w_swaps[r].wait_recv()
            for p in range(parts):

                def store(rows, j, cols, value, r=r, p=p):
                    y_send[r - 1, p, rows, pl.ds(pl.multiple_of(j * GROUP, GROUP), GROUP)] = value.astype(BF16)

                project(b, r, p * part, part // GROUP, store)
                span = pl.ds(b * BLOCK, BLOCK)
                at = (b * parts + p,)
                y_copies[b, r, p] = remote(
                    y_send.at[r - 1, p, span], y_recv.at[r - 1, p, span],
                    ys_send.at[r - 1, at[0]], ys_recv.at[r - 1, at[0]],
                    ctx, (iy + r) % n_y * 2 + core,
                )
                y_copies[b, r, p].start()

    norm(0)
    for b in range(blocks):
        if b + 1 < blocks:
            norm(b + 1)
        send_block(b)

    w_loads[0].wait()
    w_swaps[0].wait_recv()

    def keep(rows, j, cols, value):
        local[rows, cols] = value

    for b in range(blocks):
        project(b, 0, 0, owned // GROUP, keep)

    for b in range(blocks):
        rows = slice(b * BLOCK, (b + 1) * BLOCK)
        for p in range(parts):
            cols = slice(p * part, (p + 1) * part)
            total = local[rows, cols]
            for r in range(1, n_y):
                y_copies[b, r, p].wait_recv()
                total = total + y_recv[r - 1, p, rows, :].astype(F32)
            out_ref[rows, cols] = total.astype(BF16)

    @pl.when(ctx < n_ctx - 1)
    def _():
        for copy in rims:
            copy.wait_send()

    @pl.when(iz < n_z - 1)
    def _():
        for copy in z_copies:
            copy.wait_send()

    for copies in (w_swaps.values(), x_copies.values(), n_copies, y_copies.values()):
        for copy in copies:
            copy.wait_send()


def solution(mesh):
    n_ctx, n_tp = mesh.shape["ctx"], mesh.shape["tp"]
    n_x = max(1, n_ctx // 4)

    def body(x_in, bc_in, z_in, codes, head_rate, conv_x, conv_bc, bias_x, bias_bc, skip, norm_gain, w_out):
        toks, width = x_in.shape
        maps = bc_in.shape[1]
        n_state = maps // 2
        depth, model = w_out.shape
        owned = model // n_tp
        part = min(owned, 1024)
        n_y = n_tp // 2
        far = max(1, n_y - 1)
        row = max(1, n_x - 1)
        groups = width // GROUP
        blocks = toks // BLOCK
        vmem = pl.BlockSpec(memory_space=pltpu.VMEM)
        smem = pl.BlockSpec(memory_space=pltpu.SMEM)
        dma = pltpu.SemaphoreType.DMA
        pieces = blocks * (owned // part)
        return pl.pallas_call(
            functools.partial(layer, n_ctx, n_tp, n_x),
            out_shape=jax.ShapeDtypeStruct((toks, owned), BF16),
            in_specs=[vmem, vmem, vmem, vmem, smem, vmem, vmem, vmem, vmem, smem, vmem,
                      pl.BlockSpec(memory_space=pl.ANY)],
            out_specs=vmem,
            scratch_shapes=[
                pltpu.VMEM((RIM, width), BF16),
                pltpu.VMEM((RIM, maps), BF16),
                pltpu.VMEM((toks, toks), BF16),
                pltpu.VMEM((toks, width), BF16),
                pltpu.VMEM((8, width), F32),
                pltpu.VMEM((8, width), F32),
                pltpu.VMEM((toks, width), F32),
                pltpu.VMEM((toks, width), F32),
                pltpu.VMEM((toks, maps), BF16),
                pltpu.VMEM((n_state, toks), BF16),
                pltpu.VMEM((toks, width), BF16),
                pltpu.VMEM((toks, width), BF16),
                pltpu.VMEM((n_x, n_state + RIM, width), BF16),
                pltpu.VMEM((n_state, width), BF16),
                pltpu.VMEM((n_state, width), BF16),
                pltpu.VMEM((n_state, width), BF16),
                pltpu.VMEM((toks, width), F32),
                pltpu.VMEM((toks, width), F32),
                pltpu.VMEM((toks, width), BF16),
                pltpu.VMEM((toks, width), BF16),
                pltpu.VMEM((n_y, depth, owned), BF16),
                pltpu.VMEM((n_y, depth, owned), BF16),
                pltpu.VMEM((far, owned // part, toks, part), BF16),
                pltpu.VMEM((far, owned // part, toks, part), BF16),
                pltpu.VMEM((toks, owned), F32),
                dma((2,)), dma((2,)),
                dma((n_y,)), dma((n_y,)), dma((n_y,)),
                dma((row, groups)), dma((row, groups)),
                dma((groups,)), dma((groups,)),
                dma((blocks,)), dma((blocks,)),
                dma((far, pieces)), dma((far, pieces)),
            ],
            compiler_params=pltpu.CompilerParams(
                collective_id=0, has_side_effects=True, vmem_limit_bytes=60 * 1024 * 1024
            ),
        )(x_in, bc_in, z_in, codes, head_rate, conv_x, conv_bc, bias_x[None], bias_bc[None], skip,
          norm_gain[None], w_out)

    in_specs = (
        P("ctx", "tp"), P("ctx", None), P("ctx", "tp"), P("ctx", "tp"), P("tp"), P(None, "tp"),
        P(), P("tp"), P(), P("tp"), P("tp"), P("tp", None),
    )
    return jax.shard_map(body, mesh=mesh, in_specs=in_specs, out_specs=P("ctx", "tp"), check_vma=False)
```

```python
import functools
import math

import jax
import jax.numpy as jnp
from jax import lax
from jax.experimental import pallas as pl
from jax.experimental.pallas import tpu as pltpu
from jax.sharding import PartitionSpec as P

MESH = pl.DeviceIdType.MESH
F32 = jnp.float32
BF16 = jnp.bfloat16
BLOCK = 128
GROUP = 256
RIM = 16


def silu(v):
    return v / (1.0 + jnp.exp(-v))


def conv(window, taps, bias):
    total = bias + taps[3:4] * window[RIM:]
    for k in range(3):
        total = total + taps[k : k + 1] * pltpu.roll(window, 3 - k, 0)[RIM:]
    return silu(total).astype(BF16)


def layer(
    n_ctx,
    n_tp,
    n_x,
    x_hbm, bc_ref, z_hbm, codes_ref, rate_ref, cx_ref, cbc_ref, bx_ref, bbc_ref, skip_ref, gain_ref, w_ref,
    out_ref,
    x_ref, z_ref, pm, rim_x, rim_bc, tril, coded, coef, skips, ec, en, bcc, bt, xc, us, states, pz, pz_next, pin,
    g_all, h_all, own_n, sib_n, w_own, w_sib, y_send, y_recv, local,
    xl_sem, zl_sem, rim_send, rim_recv, wl_sem, ws_send, ws_recv, x_send, x_recv, z_send, z_recv, n_send, n_recv, ys_send, ys_recv,
):
    toks, width = x_hbm.shape
    heads = skip_ref.shape[0]
    n_z = n_ctx // n_x
    n_y = n_tp // 2
    blocks = toks // BLOCK
    groups = width // GROUP
    owned = out_ref.shape[1]
    part = y_send.shape[3]
    parts = owned // part
    ctx = lax.axis_index("ctx")
    tp = lax.axis_index("tp")
    iz, ix = ctx // n_x, ctx % n_x
    iy, core = tp // 2, tp % 2
    sib = tp + 1 - 2 * core
    seq = toks * n_ctx
    n_state = bc_ref.shape[1] // 2

    barrier = pltpu.get_barrier_semaphore()

    def greet(c, t):
        pl.semaphore_signal(barrier, inc=1, device_id=(c, t), device_id_type=MESH)

    greet(ctx, sib)
    for r in range(1, n_y):
        greet(ctx, (iy + r) % n_y * 2 + core)
    for r in range(1, n_x):
        greet(iz * n_x + (ix + r) % n_x, tp)
    for near, far in ((ctx > 0, ctx - 1), (ctx < n_ctx - 1, ctx + 1), (iz > 0, ctx - n_x), (iz < n_z - 1, ctx + n_x)):
        pl.when(near)(functools.partial(greet, far, tp))
    count = n_y + n_x - 1
    for near in (ctx > 0, ctx < n_ctx - 1, iz > 0, iz < n_z - 1):
        count = count + jnp.where(near, 1, 0)

    def remote(src, dst, send, recv, c, t):
        return pltpu.make_async_remote_copy(
            src_ref=src, dst_ref=dst, send_sem=send, recv_sem=recv, device_id=(c, t), device_id_type=MESH
        )

    def span_of(g):
        return pl.ds(pl.multiple_of(g * GROUP, GROUP), GROUP)

    def load_x(g):
        return pltpu.make_async_copy(x_hbm.at[:, span_of(g)], x_ref.at[:, span_of(g)], xl_sem.at[g])

    load_z = pltpu.make_async_copy(z_hbm, z_ref, zl_sem.at[0])
    for g in range(groups):
        load_x(g).start()
    load_z.start()

    row_id = lax.broadcasted_iota(jnp.int32, (toks, toks), 0)
    col_id = lax.broadcasted_iota(jnp.int32, (toks, toks), 1)
    tril[...] = jnp.where(row_id >= col_id, 1.0, 0.0).astype(BF16)
    codes = codes_ref[...].astype(F32).T
    for h in range(heads):
        cols = slice(h * BLOCK, (h + 1) * BLOCK)
        coded[:, cols] = jnp.broadcast_to(codes[:, h : h + 1], (toks, BLOCK)).astype(BF16)
        coef[:, cols] = jnp.full((8, BLOCK), rate_ref[h] * (-12.288 / seq / 63.0), F32)
        skips[:, cols] = jnp.full((8, BLOCK), skip_ref[h], F32)

    pl.semaphore_wait(barrier, count)

    rims = [
        remote(x_hbm.at[pl.ds(toks - RIM, RIM)], rim_x, rim_send.at[0], rim_recv.at[0], ctx + 1, tp),
        remote(bc_ref.at[pl.ds(toks - RIM, RIM)], rim_bc, rim_send.at[1], rim_recv.at[1], ctx + 1, tp),
    ]

    @pl.when(ctx < n_ctx - 1)
    def _():
        for copy in rims:
            copy.start()

    order = list(range(1, n_y)) + [0]
    w_loads, w_swaps = {}, {}
    for r in order:
        chip = (iy + r) % n_y
        mine = pl.ds(pl.multiple_of((chip * 2 + core) * owned, GROUP), owned)
        theirs = pl.ds(pl.multiple_of((chip * 2 + 1 - core) * owned, GROUP), owned)
        w_loads[r] = pltpu.make_async_copy(w_ref.at[:, mine], w_own.at[r], wl_sem.at[r])
        w_swaps[r] = remote(w_ref.at[:, theirs], w_sib.at[r], ws_send.at[r], ws_recv.at[r], ctx, sib)
        w_loads[r].start()
        w_swaps[r].start()

    def decays(j, _):
        cols = span_of(j)
        cum = jnp.dot(tril[...], coded[:, cols], preferred_element_type=F32) * coef[0:1, cols]
        ec[:, cols] = jnp.exp(cum)
        en[:, cols] = jnp.exp(-cum)
        return 0

    lax.fori_loop(0, groups, decays, 0)

    def conv_bc(b):
        rows = pl.ds(b * BLOCK, BLOCK)
        if b == 0:
            window = jnp.concatenate([rim_bc[...], bc_ref[rows, :]], axis=0)
        else:
            window = bc_ref[pl.ds(b * BLOCK - RIM, BLOCK + RIM), :]
        value = conv(window.astype(F32), cbc_ref[...], bbc_ref[...])
        bcc[rows, :] = value
        bt[:, b * BLOCK : (b + 1) * BLOCK] = value[:, :n_state].astype(F32).T.astype(BF16)

    for b in range(1, blocks):
        conv_bc(b)

    @pl.when(ctx == 0)
    def _():
        rim_x[...] = jnp.zeros_like(rim_x)
        rim_bc[...] = jnp.zeros_like(rim_bc)

    @pl.when(ctx > 0)
    def _():
        for copy in rims:
            copy.wait_recv()

    conv_bc(0)

    @pl.when(iz == 0)
    def _():
        pz[...] = jnp.zeros_like(pz)

    def x_copy(r, g):
        return remote(
            states.at[n_x - 1, :, span_of(g)], states.at[r - 1, :, span_of(g)],
            x_send.at[r - 1, g], x_recv.at[r - 1, g],
            iz * n_x + (ix + r) % n_x, tp,
        )

    def z_copy(g):
        return remote(pz_next.at[:, span_of(g)], pz.at[:, span_of(g)], z_send.at[g], z_recv.at[g], ctx + n_x, tp)

    def n_copy(g):
        return remote(own_n.at[:, span_of(g)], sib_n.at[:, span_of(g)], n_send.at[g], n_recv.at[g], ctx, sib)

    def own_state(g):
        load_x(g).wait()
        for half in range(GROUP // BLOCK):
            cols = pl.ds(pl.multiple_of(g * GROUP + half * BLOCK, BLOCK), BLOCK)
            for b in range(blocks):
                rows = pl.ds(b * BLOCK, BLOCK)
                if b == 0:
                    window = jnp.concatenate([rim_x[:, cols], x_ref[rows, cols]], axis=0)
                else:
                    window = x_ref[pl.ds(b * BLOCK - RIM, BLOCK + RIM), cols]
                value = conv(window.astype(F32), cx_ref[:, cols], bx_ref[:, cols])
                xc[rows, cols] = value
                us[rows, cols] = (value.astype(F32) * en[rows, cols]).astype(BF16)
        cols = span_of(g)
        total = ec[toks - 1 : toks, cols]
        state = jnp.dot(bt[...], us[:, cols], preferred_element_type=F32)
        states[n_x - 1, :n_state, cols] = (state * total).astype(BF16)
        high = total.astype(BF16).astype(F32)
        pick = lax.broadcasted_iota(jnp.int32, (RIM, GROUP), 0) < 8
        states[n_x - 1, n_state:, cols] = jnp.where(pick, high, total - high).astype(BF16)
        for r in range(1, n_x):
            x_copy(r, g).start()

    def score():
        load_z.wait()
        for b in range(blocks):
            rows = slice(b * BLOCK, (b + 1) * BLOCK)
            upto = (b + 1) * BLOCK
            scores = lax.dot_general(
                bcc[rows, n_state:], bcc[:upto, :n_state], (((1,), (1,)), ((), ())), preferred_element_type=F32
            )
            pm[rows, :upto] = (scores * tril[rows, :upto].astype(F32)).astype(BF16)

    scale = 1.0 / math.sqrt(n_state * seq)

    def inside(g):
        cols = span_of(g)
        for b in range(blocks):
            rows = slice(b * BLOCK, (b + 1) * BLOCK)
            upto = (b + 1) * BLOCK
            y = jnp.dot(pm[rows, :upto], us[:upto, cols], preferred_element_type=F32)
            gate = silu(z_ref[rows, cols].astype(F32))
            decay = ec[rows, cols] * (scale * gate)
            g_all[rows, cols] = y * decay + skips[0:1, cols] * xc[rows, cols].astype(F32) * gate
            h_all[rows, cols] = decay

    def prefix(g):
        cols = span_of(g)
        for r in range(1, n_x):
            x_copy(r, g).wait_recv()
        pl.when(iz > 0)(lambda: z_copy(g).wait_recv())
        before = pz[:, cols].astype(F32)
        arrived = before
        for k in range(n_x):
            slot = (ix - k - 1 + n_x) % n_x
            arrived = jnp.where(ix == k, before, arrived)
            factor = states[slot, n_state : n_state + 1, cols].astype(F32)
            factor = factor + states[slot, n_state + 8 : n_state + 9, cols].astype(F32)
            before = before * factor + states[slot, :n_state, cols].astype(F32)
        pz_next[:, cols] = before.astype(BF16)
        pl.when(iz < n_z - 1)(lambda: z_copy(g).start())
        pin[:, cols] = arrived.astype(BF16)

    def norm(g):
        cols = span_of(g)
        for b in range(blocks):
            rows = slice(b * BLOCK, (b + 1) * BLOCK)
            carried = jnp.dot(bcc[rows, n_state:], pin[:, cols], preferred_element_type=F32)
            gated = g_all[rows, cols] + h_all[rows, cols] * carried
            for half in range(GROUP // BLOCK):
                piece = gated[:, half * BLOCK : (half + 1) * BLOCK]
                mean_square = jnp.mean(piece * piece, axis=-1, keepdims=True)
                cut = pl.ds(pl.multiple_of(g * GROUP + half * BLOCK, BLOCK), BLOCK)
                own_n[rows, cut] = (piece * lax.rsqrt(mean_square + 1e-05) * gain_ref[:, cut]).astype(BF16)
        n_copy(g).start()

    delay = jnp.where(iz == n_z - 1, 2 * groups - 1, iz + 1)
    late = jnp.maximum(delay, groups)

    def slot_step(s, _):
        pl.when(s < groups)(lambda: own_state(s))
        pl.when(s == groups)(score)
        pl.when((s >= groups) & (s < 2 * groups))(lambda: inside(s - groups))
        pl.when((s >= delay) & (s < delay + groups))(lambda: prefix(s - delay))
        pl.when((s >= late) & (s < late + groups))(lambda: norm(s - late))
        return 0

    lax.fori_loop(0, groups + max(2 * groups - 1, n_z), slot_step, 0)

    def project(b, r, first, tiles, store):
        rows = slice(b * BLOCK, (b + 1) * BLOCK)

        def tile(j, _):
            cols = pl.ds(pl.multiple_of(first + j * GROUP, GROUP), GROUP)
            value = jnp.dot(own_n[rows, :], w_own[r, :, cols], preferred_element_type=F32)
            value = value + jnp.dot(sib_n[rows, :], w_sib[r, :, cols], preferred_element_type=F32)
            store(rows, j, cols, value)
            return 0

        lax.fori_loop(0, tiles, tile, 0)

    y_copies = {}

    def send_block(b):
        for r in range(1, n_y):
            if b == 0:
                w_loads[r].wait()
                w_swaps[r].wait_recv()
            for p in range(parts):

                def store(rows, j, cols, value, r=r, p=p):
                    y_send[r - 1, p, rows, span_of(j)] = value.astype(BF16)

                project(b, r, p * part, part // GROUP, store)
                span = pl.ds(b * BLOCK, BLOCK)
                at = b * parts + p
                y_copies[b, r, p] = remote(
                    y_send.at[r - 1, p, span], y_recv.at[r - 1, p, span],
                    ys_send.at[r - 1, at], ys_recv.at[r - 1, at],
                    ctx, (iy + r) % n_y * 2 + core,
                )
                y_copies[b, r, p].start()

    for g in range(groups):
        n_copy(g).wait_recv()
    for b in range(blocks):
        send_block(b)

    w_loads[0].wait()
    w_swaps[0].wait_recv()

    def keep(rows, j, cols, value):
        local[rows, cols] = value

    for b in range(blocks):
        project(b, 0, 0, owned // GROUP, keep)

    for b in range(blocks):
        rows = slice(b * BLOCK, (b + 1) * BLOCK)
        for p in range(parts):
            cols = slice(p * part, (p + 1) * part)
            total = local[rows, cols]
            for r in range(1, n_y):
                y_copies[b, r, p].wait_recv()
                total = total + y_recv[r - 1, p, rows, :].astype(F32)
            out_ref[rows, cols] = total.astype(BF16)

    @pl.when(ctx < n_ctx - 1)
    def _():
        for copy in rims:
            copy.wait_send()

    @pl.when(iz < n_z - 1)
    def _():
        for g in range(groups):
            z_copy(g).wait_send()

    for g in range(groups):
        n_copy(g).wait_send()
        for r in range(1, n_x):
            x_copy(r, g).wait_send()
    for copies in (w_swaps.values(), y_copies.values()):
        for copy in copies:
            copy.wait_send()


def solution(mesh):
    n_ctx, n_tp = mesh.shape["ctx"], mesh.shape["tp"]
    n_x = max(1, n_ctx // 4)

    def body(x_in, bc_in, z_in, codes, head_rate, conv_x, conv_bc, bias_x, bias_bc, skip, norm_gain, w_out):
        toks, width = x_in.shape
        maps = bc_in.shape[1]
        n_state = maps // 2
        depth, model = w_out.shape
        owned = model // n_tp
        part = min(owned, 1024)
        n_y = n_tp // 2
        far = max(1, n_y - 1)
        row = max(1, n_x - 1)
        groups = width // GROUP
        blocks = toks // BLOCK
        vmem = pl.BlockSpec(memory_space=pltpu.VMEM)
        hbm = pl.BlockSpec(memory_space=pl.ANY)
        smem = pl.BlockSpec(memory_space=pltpu.SMEM)
        dma = pltpu.SemaphoreType.DMA
        pieces = blocks * (owned // part)
        return pl.pallas_call(
            functools.partial(layer, n_ctx, n_tp, n_x),
            out_shape=jax.ShapeDtypeStruct((toks, owned), BF16),
            in_specs=[hbm, vmem, hbm, vmem, smem, vmem, vmem, vmem, vmem, smem, vmem, hbm],
            out_specs=vmem,
            scratch_shapes=[
                pltpu.VMEM((toks, width), BF16),
                pltpu.VMEM((toks, width), BF16),
                pltpu.VMEM((toks, toks), BF16),
                pltpu.VMEM((RIM, width), BF16),
                pltpu.VMEM((RIM, maps), BF16),
                pltpu.VMEM((toks, toks), BF16),
                pltpu.VMEM((toks, width), BF16),
                pltpu.VMEM((8, width), F32),
                pltpu.VMEM((8, width), F32),
                pltpu.VMEM((toks, width), F32),
                pltpu.VMEM((toks, width), F32),
                pltpu.VMEM((toks, maps), BF16),
                pltpu.VMEM((n_state, toks), BF16),
                pltpu.VMEM((toks, width), BF16),
                pltpu.VMEM((toks, width), BF16),
                pltpu.VMEM((n_x, n_state + RIM, width), BF16),
                pltpu.VMEM((n_state, width), BF16),
                pltpu.VMEM((n_state, width), BF16),
                pltpu.VMEM((n_state, width), BF16),
                pltpu.VMEM((toks, width), F32),
                pltpu.VMEM((toks, width), F32),
                pltpu.VMEM((toks, width), BF16),
                pltpu.VMEM((toks, width), BF16),
                pltpu.VMEM((n_y, depth, owned), BF16),
                pltpu.VMEM((n_y, depth, owned), BF16),
                pltpu.VMEM((far, owned // part, toks, part), BF16),
                pltpu.VMEM((far, owned // part, toks, part), BF16),
                pltpu.VMEM((toks, owned), F32),
                dma((groups,)), dma((1,)), dma((2,)), dma((2,)),
                dma((n_y,)), dma((n_y,)), dma((n_y,)),
                dma((row, groups)), dma((row, groups)),
                dma((groups,)), dma((groups,)),
                dma((groups,)), dma((groups,)),
                dma((far, pieces)), dma((far, pieces)),
            ],
            compiler_params=pltpu.CompilerParams(
                collective_id=0, has_side_effects=True, vmem_limit_bytes=60 * 1024 * 1024
            ),
        )(x_in, bc_in, z_in, codes.T, head_rate, conv_x, conv_bc, bias_x[None], bias_bc[None], skip,
          norm_gain[None], w_out)

    in_specs = (
        P("ctx", "tp"), P("ctx", None), P("ctx", "tp"), P("ctx", "tp"), P("tp"), P(None, "tp"),
        P(), P("tp"), P(), P("tp"), P("tp"), P("tp", None),
    )
    return jax.shard_map(body, mesh=mesh, in_specs=in_specs, out_specs=P("ctx", "tp"), check_vma=False)
```

```python
import functools
import math

import jax
import jax.numpy as jnp
from jax import lax
from jax.experimental import pallas as pl
from jax.experimental.pallas import tpu as pltpu
from jax.sharding import PartitionSpec as P

MESH = pl.DeviceIdType.MESH
F32 = jnp.float32
BF16 = jnp.bfloat16
BLOCK = 128
GROUP = 256
RIM = 16


def silu(v):
    half = 0.5 * v
    return half + half * jnp.tanh(half)


def conv(window, taps, bias):
    total = bias + taps[3:4] * window[RIM:]
    for k in range(3):
        total = total + taps[k : k + 1] * pltpu.roll(window, 3 - k, 0)[RIM:]
    return silu(total).astype(BF16)


def layer(
    n_ctx,
    n_tp,
    n_x,
    x_hbm, bc_ref, z_hbm, codes_ref, rate_ref, cx_ref, cbc_ref, bx_ref, bbc_ref, skip_ref, gain_ref, w_ref,
    out_ref,
    x_ref, z_ref, pm, rim_x, rim_bc, tril, coded, coef, skips, ec, en, bcc, bt, xc, us, states, pz, pz_next, pin,
    g_all, h_all, own_n, sib_n, w_own, w_sib, y_send, y_recv, local,
    xl_sem, zl_sem, rim_send, rim_recv, wl_sem, ws_send, ws_recv, x_send, x_recv, z_send, z_recv, n_send, n_recv, ys_send, ys_recv,
):
    toks, width = x_hbm.shape
    heads = skip_ref.shape[0]
    n_z = n_ctx // n_x
    n_y = n_tp // 2
    blocks = toks // BLOCK
    groups = width // GROUP
    owned = out_ref.shape[1]
    part = y_send.shape[3]
    parts = owned // part
    ctx = lax.axis_index("ctx")
    tp = lax.axis_index("tp")
    iz, ix = ctx // n_x, ctx % n_x
    iy, core = tp // 2, tp % 2
    sib = tp + 1 - 2 * core
    seq = toks * n_ctx
    n_state = bc_ref.shape[1] // 2

    barrier = pltpu.get_barrier_semaphore()

    def greet(c, t):
        pl.semaphore_signal(barrier, inc=1, device_id=(c, t), device_id_type=MESH)

    greet(ctx, sib)
    for r in range(1, n_y):
        greet(ctx, (iy + r) % n_y * 2 + core)
    for r in range(1, n_x):
        greet(iz * n_x + (ix + r) % n_x, tp)
    for near, far in ((ctx > 0, ctx - 1), (ctx < n_ctx - 1, ctx + 1), (iz > 0, ctx - n_x), (iz < n_z - 1, ctx + n_x)):
        pl.when(near)(functools.partial(greet, far, tp))
    count = n_y + n_x - 1
    for near in (ctx > 0, ctx < n_ctx - 1, iz > 0, iz < n_z - 1):
        count = count + jnp.where(near, 1, 0)

    def remote(src, dst, send, recv, c, t):
        return pltpu.make_async_remote_copy(
            src_ref=src, dst_ref=dst, send_sem=send, recv_sem=recv, device_id=(c, t), device_id_type=MESH
        )

    def span_of(g):
        return pl.ds(pl.multiple_of(g * GROUP, GROUP), GROUP)

    def load_x(g):
        return pltpu.make_async_copy(x_hbm.at[:, span_of(g)], x_ref.at[:, span_of(g)], xl_sem.at[g])

    load_z = pltpu.make_async_copy(z_hbm, z_ref, zl_sem.at[0])
    for g in range(groups):
        load_x(g).start()
    load_z.start()

    row_id = lax.broadcasted_iota(jnp.int32, (toks, toks), 0)
    col_id = lax.broadcasted_iota(jnp.int32, (toks, toks), 1)
    tril[...] = jnp.where(row_id >= col_id, 1.0, 0.0).astype(BF16)
    codes = codes_ref[...].astype(F32).T
    for h in range(heads):
        cols = slice(h * BLOCK, (h + 1) * BLOCK)
        coded[:, cols] = jnp.broadcast_to(codes[:, h : h + 1], (toks, BLOCK)).astype(BF16)
        coef[:, cols] = jnp.full((8, BLOCK), rate_ref[h] * (-12.288 / seq / 63.0), F32)
        skips[:, cols] = jnp.full((8, BLOCK), skip_ref[h], F32)

    pl.semaphore_wait(barrier, count)

    rims = [
        remote(x_hbm.at[pl.ds(toks - RIM, RIM)], rim_x, rim_send.at[0], rim_recv.at[0], ctx + 1, tp),
        remote(bc_ref.at[pl.ds(toks - RIM, RIM)], rim_bc, rim_send.at[1], rim_recv.at[1], ctx + 1, tp),
    ]

    @pl.when(ctx < n_ctx - 1)
    def _():
        for copy in rims:
            copy.start()

    order = list(range(1, n_y)) + [0]
    w_loads, w_swaps = {}, {}
    for r in order:
        chip = (iy + r) % n_y
        mine = pl.ds(pl.multiple_of((chip * 2 + core) * owned, GROUP), owned)
        theirs = pl.ds(pl.multiple_of((chip * 2 + 1 - core) * owned, GROUP), owned)
        w_loads[r] = pltpu.make_async_copy(w_ref.at[:, mine], w_own.at[r], wl_sem.at[r])
        w_swaps[r] = remote(w_ref.at[:, theirs], w_sib.at[r], ws_send.at[r], ws_recv.at[r], ctx, sib)
        w_loads[r].start()
        w_swaps[r].start()

    def decays(j, _):
        cols = span_of(j)
        cum = jnp.dot(tril[...], coded[:, cols], preferred_element_type=F32) * coef[0:1, cols]
        ec[:, cols] = jnp.exp(cum)
        en[:, cols] = jnp.exp(-cum)
        return 0

    lax.fori_loop(0, groups, decays, 0)

    def conv_bc(b):
        rows = pl.ds(b * BLOCK, BLOCK)
        if b == 0:
            window = jnp.concatenate([rim_bc[...], bc_ref[rows, :]], axis=0)
        else:
            window = bc_ref[pl.ds(b * BLOCK - RIM, BLOCK + RIM), :]
        value = conv(window.astype(F32), cbc_ref[...], bbc_ref[...])
        bcc[rows, :] = value
        bt[:, b * BLOCK : (b + 1) * BLOCK] = value[:, :n_state].astype(F32).T.astype(BF16)

    for b in range(1, blocks):
        conv_bc(b)

    @pl.when(ctx == 0)
    def _():
        rim_x[...] = jnp.zeros_like(rim_x)
        rim_bc[...] = jnp.zeros_like(rim_bc)

    @pl.when(ctx > 0)
    def _():
        for copy in rims:
            copy.wait_recv()

    conv_bc(0)

    @pl.when(iz == 0)
    def _():
        pz[...] = jnp.zeros_like(pz)

    def strip_of(q):
        return pl.ds(pl.multiple_of(q * BLOCK, BLOCK), BLOCK)

    def x_copy(r, q):
        return remote(
            states.at[n_x - 1, :, strip_of(q)], states.at[r - 1, :, strip_of(q)],
            x_send.at[r - 1, q], x_recv.at[r - 1, q],
            iz * n_x + (ix + r) % n_x, tp,
        )

    def z_copy(q):
        return remote(pz_next.at[:, strip_of(q)], pz.at[:, strip_of(q)], z_send.at[q], z_recv.at[q], ctx + n_x, tp)

    def n_copy(g, b):
        rows = pl.ds(b * BLOCK, BLOCK)
        return remote(own_n.at[rows, span_of(g)], sib_n.at[rows, span_of(g)], n_send.at[g, b], n_recv.at[g, b], ctx, sib)

    def own_state(g):
        load_x(g).wait()
        for half in range(GROUP // BLOCK):
            cols = pl.ds(pl.multiple_of(g * GROUP + half * BLOCK, BLOCK), BLOCK)
            for b in range(blocks):
                rows = pl.ds(b * BLOCK, BLOCK)
                if b == 0:
                    window = jnp.concatenate([rim_x[:, cols], x_ref[rows, cols]], axis=0)
                else:
                    window = x_ref[pl.ds(b * BLOCK - RIM, BLOCK + RIM), cols]
                value = conv(window.astype(F32), cx_ref[:, cols], bx_ref[:, cols])
                xc[rows, cols] = value
                us[rows, cols] = (value.astype(F32) * en[rows, cols]).astype(BF16)
        cols = span_of(g)
        total = ec[toks - 1 : toks, cols]
        state = jnp.dot(bt[...], us[:, cols], preferred_element_type=F32)
        states[n_x - 1, :n_state, cols] = (state * total).astype(BF16)
        high = total.astype(BF16).astype(F32)
        pick = lax.broadcasted_iota(jnp.int32, (RIM, GROUP), 0) < 8
        states[n_x - 1, n_state:, cols] = jnp.where(pick, high, total - high).astype(BF16)
        for half in range(GROUP // BLOCK):
            for r in range(1, n_x):
                x_copy(r, g * (GROUP // BLOCK) + half).start()

    def score():
        load_z.wait()
        for b in range(blocks):
            rows = slice(b * BLOCK, (b + 1) * BLOCK)
            upto = (b + 1) * BLOCK
            scores = lax.dot_general(
                bcc[rows, n_state:], bcc[:upto, :n_state], (((1,), (1,)), ((), ())), preferred_element_type=F32
            )
            pm[rows, :upto] = (scores * tril[rows, :upto].astype(F32)).astype(BF16)

    scale = 1.0 / math.sqrt(n_state * seq)

    def inside(g):
        cols = span_of(g)
        for b in range(blocks):
            rows = slice(b * BLOCK, (b + 1) * BLOCK)
            upto = (b + 1) * BLOCK
            y = jnp.dot(pm[rows, :upto], us[:upto, cols], preferred_element_type=F32)
            gate = silu(z_ref[rows, cols].astype(F32))
            decay = ec[rows, cols] * (scale * gate)
            g_all[rows, cols] = y * decay + skips[0:1, cols] * xc[rows, cols].astype(F32) * gate
            h_all[rows, cols] = decay

    def prefix(g):
        for half in range(GROUP // BLOCK):
            q = g * (GROUP // BLOCK) + half
            cols = strip_of(q)
            for r in range(1, n_x):
                x_copy(r, q).wait_recv()
            pl.when(iz > 0)(functools.partial(lambda q: z_copy(q).wait_recv(), q))
            before = pz[:, cols].astype(F32)
            arrived = before
            for k in range(n_x):
                slot = (ix - k - 1 + n_x) % n_x
                arrived = jnp.where(ix == k, before, arrived)
                factor = states[slot, n_state : n_state + 1, cols].astype(F32)
                factor = factor + states[slot, n_state + 8 : n_state + 9, cols].astype(F32)
                before = before * factor + states[slot, :n_state, cols].astype(F32)
            pz_next[:, cols] = before.astype(BF16)
            pl.when(iz < n_z - 1)(functools.partial(lambda q: z_copy(q).start(), q))
            pin[:, cols] = arrived.astype(BF16)

    def norm(g):
        cols = span_of(g)
        for b in range(blocks):
            rows = slice(b * BLOCK, (b + 1) * BLOCK)
            carried = jnp.dot(bcc[rows, n_state:], pin[:, cols], preferred_element_type=F32)
            gated = g_all[rows, cols] + h_all[rows, cols] * carried
            for half in range(GROUP // BLOCK):
                piece = gated[:, half * BLOCK : (half + 1) * BLOCK]
                mean_square = jnp.mean(piece * piece, axis=-1, keepdims=True)
                cut = pl.ds(pl.multiple_of(g * GROUP + half * BLOCK, BLOCK), BLOCK)
                own_n[rows, cut] = (piece * lax.rsqrt(mean_square + 1e-05) * gain_ref[:, cut]).astype(BF16)
            n_copy(g, b).start()

    delay = jnp.where(iz == n_z - 1, 2 * groups - 1, iz + 1)
    late = jnp.maximum(delay, groups)

    def slot_step(s, _):
        pl.when(s < groups)(lambda: own_state(s))
        pl.when(s == groups)(score)
        pl.when((s >= groups) & (s < 2 * groups))(lambda: inside(s - groups))
        pl.when((s >= delay) & (s < delay + groups))(lambda: prefix(s - delay))
        pl.when((s >= late) & (s < late + groups))(lambda: norm(s - late))
        return 0

    lax.fori_loop(0, groups + max(2 * groups - 1, n_z), slot_step, 0)

    def project(b, r, first, tiles, store):
        rows = slice(b * BLOCK, (b + 1) * BLOCK)

        def tile(j, _):
            cols = pl.ds(pl.multiple_of(first + j * GROUP, GROUP), GROUP)
            value = jnp.dot(own_n[rows, :], w_own[r, :, cols], preferred_element_type=F32)
            value = value + jnp.dot(sib_n[rows, :], w_sib[r, :, cols], preferred_element_type=F32)
            store(rows, j, cols, value)
            return 0

        lax.fori_loop(0, tiles, tile, 0)

    y_copies = {}

    def send_block(b):
        for r in range(1, n_y):
            if b == 0:
                w_loads[r].wait()
                w_swaps[r].wait_recv()
            for p in range(parts):

                def store(rows, j, cols, value, r=r, p=p):
                    y_send[r - 1, p, rows, span_of(j)] = value.astype(BF16)

                project(b, r, p * part, part // GROUP, store)
                span = pl.ds(b * BLOCK, BLOCK)
                at = b * parts + p
                y_copies[b, r, p] = remote(
                    y_send.at[r - 1, p, span], y_recv.at[r - 1, p, span],
                    ys_send.at[r - 1, at], ys_recv.at[r - 1, at],
                    ctx, (iy + r) % n_y * 2 + core,
                )
                y_copies[b, r, p].start()

    for b in range(blocks):
        for g in range(groups):
            n_copy(g, b).wait_recv()
        send_block(b)

    w_loads[0].wait()
    w_swaps[0].wait_recv()

    def keep(rows, j, cols, value):
        local[rows, cols] = value

    for b in range(blocks):
        project(b, 0, 0, owned // GROUP, keep)

    for b in range(blocks):
        rows = slice(b * BLOCK, (b + 1) * BLOCK)
        for p in range(parts):
            cols = slice(p * part, (p + 1) * part)
            total = local[rows, cols]
            for r in range(1, n_y):
                y_copies[b, r, p].wait_recv()
                total = total + y_recv[r - 1, p, rows, :].astype(F32)
            out_ref[rows, cols] = total.astype(BF16)

    @pl.when(ctx < n_ctx - 1)
    def _():
        for copy in rims:
            copy.wait_send()

    @pl.when(iz < n_z - 1)
    def _():
        for q in range(width // BLOCK):
            z_copy(q).wait_send()

    for g in range(groups):
        for b in range(blocks):
            n_copy(g, b).wait_send()
    for q in range(width // BLOCK):
        for r in range(1, n_x):
            x_copy(r, q).wait_send()
    for copies in (w_swaps.values(), y_copies.values()):
        for copy in copies:
            copy.wait_send()


def hand_on(from_ref, to_ref, sem):
    count = sem.shape[0]
    rows = from_ref.shape[0] // count
    copies = []
    for k in range(count):
        span = pl.ds(k * rows, rows)
        copies.append(pltpu.make_async_copy(from_ref.at[span], to_ref.at[span], sem.at[k]))
    for copy in copies:
        copy.start()
    for copy in copies:
        copy.wait()


def solution(mesh):
    n_ctx, n_tp = mesh.shape["ctx"], mesh.shape["tp"]
    n_x = max(1, n_ctx // 4)

    def body(x_in, bc_in, z_in, codes, head_rate, conv_x, conv_bc, bias_x, bias_bc, skip, norm_gain, w_out):
        toks, width = x_in.shape
        maps = bc_in.shape[1]
        n_state = maps // 2
        depth, model = w_out.shape
        owned = model // n_tp
        part = min(owned, 512)
        n_y = n_tp // 2
        far = max(1, n_y - 1)
        row = max(1, n_x - 1)
        groups = width // GROUP
        strips = width // BLOCK
        blocks = toks // BLOCK
        vmem = pl.BlockSpec(memory_space=pltpu.VMEM)
        hbm = pl.BlockSpec(memory_space=pl.ANY)
        smem = pl.BlockSpec(memory_space=pltpu.SMEM)
        dma = pltpu.SemaphoreType.DMA
        pieces = blocks * (owned // part)
        result = pl.pallas_call(
            functools.partial(layer, n_ctx, n_tp, n_x),
            out_shape=pltpu.VMEM((toks, owned), BF16),
            in_specs=[hbm, vmem, hbm, vmem, smem, vmem, vmem, vmem, vmem, smem, vmem, hbm],
            out_specs=vmem,
            scratch_shapes=[
                pltpu.VMEM((toks, width), BF16),
                pltpu.VMEM((toks, width), BF16),
                pltpu.VMEM((toks, toks), BF16),
                pltpu.VMEM((RIM, width), BF16),
                pltpu.VMEM((RIM, maps), BF16),
                pltpu.VMEM((toks, toks), BF16),
                pltpu.VMEM((toks, width), BF16),
                pltpu.VMEM((8, width), F32),
                pltpu.VMEM((8, width), F32),
                pltpu.VMEM((toks, width), F32),
                pltpu.VMEM((toks, width), F32),
                pltpu.VMEM((toks, maps), BF16),
                pltpu.VMEM((n_state, toks), BF16),
                pltpu.VMEM((toks, width), BF16),
                pltpu.VMEM((toks, width), BF16),
                pltpu.VMEM((n_x, n_state + RIM, width), BF16),
                pltpu.VMEM((n_state, width), BF16),
                pltpu.VMEM((n_state, width), BF16),
                pltpu.VMEM((n_state, width), BF16),
                pltpu.VMEM((toks, width), F32),
                pltpu.VMEM((toks, width), F32),
                pltpu.VMEM((toks, width), BF16),
                pltpu.VMEM((toks, width), BF16),
                pltpu.VMEM((n_y, depth, owned), BF16),
                pltpu.VMEM((n_y, depth, owned), BF16),
                pltpu.VMEM((far, owned // part, toks, part), BF16),
                pltpu.VMEM((far, owned // part, toks, part), BF16),
                pltpu.VMEM((toks, owned), F32),
                dma((groups,)), dma((1,)), dma((2,)), dma((2,)),
                dma((n_y,)), dma((n_y,)), dma((n_y,)),
                dma((row, strips)), dma((row, strips)),
                dma((strips,)), dma((strips,)),
                dma((groups, blocks)), dma((groups, blocks)),
                dma((far, pieces)), dma((far, pieces)),
            ],
            compiler_params=pltpu.CompilerParams(
                collective_id=0, has_side_effects=True, vmem_limit_bytes=58 * 1024 * 1024
            ),
        )(x_in, bc_in, z_in, codes.T, head_rate, conv_x, conv_bc, bias_x[None], bias_bc[None], skip,
          norm_gain[None], w_out)
        return pl.pallas_call(
            hand_on,
            out_shape=jax.ShapeDtypeStruct((toks, owned), BF16),
            in_specs=[pl.BlockSpec(memory_space=pltpu.VMEM)],
            out_specs=hbm,
            scratch_shapes=[dma((8,))],
        )(result)

    in_specs = (
        P("ctx", "tp"), P("ctx", None), P("ctx", "tp"), P("ctx", "tp"), P("tp"), P(None, "tp"),
        P(), P("tp"), P(), P("tp"), P("tp"), P("tp", None),
    )
    return jax.shard_map(body, mesh=mesh, in_specs=in_specs, out_specs=P("ctx", "tp"), check_vma=False)
```

```python
import functools
import math

import jax
import jax.numpy as jnp
from jax import lax
from jax.experimental import pallas as pl
from jax.experimental.pallas import tpu as pltpu
from jax.sharding import PartitionSpec as P

MESH = pl.DeviceIdType.MESH
F32 = jnp.float32
BF16 = jnp.bfloat16
BLOCK = 128
GROUP = 256
RIM = 16


def silu(v):
    half = 0.5 * v
    return half + half * jnp.tanh(half)


def conv(window, taps, bias):
    total = bias + taps[3:4] * window[RIM:]
    for k in range(3):
        total = total + taps[k : k + 1] * pltpu.roll(window, 3 - k, 0)[RIM:]
    return silu(total).astype(BF16)


def layer(
    n_ctx,
    n_tp,
    n_x,
    x_hbm, bc_ref, z_hbm, codes_ref, rate_ref, cx_ref, cbc_ref, bx_ref, bbc_ref, skip_ref, gain_ref, w_ref,
    out_ref,
    x_ref, z_ref, pm, rim_x, rim_bc, tril, coded, coef, skips, ec, en, bcc, bt, xc, us, states, pz, pz_next, pin,
    g_all, h_all, own_n, sib_n, w_own, w_sib, y_send, y_recv, local,
    xl_sem, zl_sem, rim_send, rim_recv, wl_sem, ws_send, ws_recv, x_send, x_recv, z_send, z_recv, n_send, n_recv, ys_send, ys_recv,
):
    toks, width = x_hbm.shape
    heads = skip_ref.shape[0]
    n_z = n_ctx // n_x
    n_y = n_tp // 2
    blocks = toks // BLOCK
    groups = width // GROUP
    owned = out_ref.shape[1]
    part = y_send.shape[3]
    parts = owned // part
    ctx = lax.axis_index("ctx")
    tp = lax.axis_index("tp")
    iz, ix = ctx // n_x, ctx % n_x
    iy, core = tp // 2, tp % 2
    sib = tp + 1 - 2 * core
    seq = toks * n_ctx
    n_state = bc_ref.shape[1] // 2

    barrier = pltpu.get_barrier_semaphore()

    def greet(c, t):
        pl.semaphore_signal(barrier, inc=1, device_id=(c, t), device_id_type=MESH)

    greet(ctx, sib)
    for r in range(1, n_y):
        greet(ctx, (iy + r) % n_y * 2 + core)
    for r in range(1, n_x):
        greet(iz * n_x + (ix + r) % n_x, tp)
    for near, far in ((ctx > 0, ctx - 1), (ctx < n_ctx - 1, ctx + 1), (iz > 0, ctx - n_x), (iz < n_z - 1, ctx + n_x)):
        pl.when(near)(functools.partial(greet, far, tp))
    count = n_y + n_x - 1
    for near in (ctx > 0, ctx < n_ctx - 1, iz > 0, iz < n_z - 1):
        count = count + jnp.where(near, 1, 0)

    def remote(src, dst, send, recv, c, t):
        return pltpu.make_async_remote_copy(
            src_ref=src, dst_ref=dst, send_sem=send, recv_sem=recv, device_id=(c, t), device_id_type=MESH
        )

    def span_of(g):
        return pl.ds(pl.multiple_of(g * GROUP, GROUP), GROUP)

    def load_x(g):
        return pltpu.make_async_copy(x_hbm.at[:, span_of(g)], x_ref.at[:, span_of(g)], xl_sem.at[g])

    load_z = pltpu.make_async_copy(z_hbm, z_ref, zl_sem.at[0])
    for g in range(groups):
        load_x(g).start()
    load_z.start()

    row_id = lax.broadcasted_iota(jnp.int32, (toks, toks), 0)
    col_id = lax.broadcasted_iota(jnp.int32, (toks, toks), 1)
    tril[...] = jnp.where(row_id >= col_id, 1.0, 0.0).astype(BF16)
    codes = codes_ref[...].astype(F32).T
    for h in range(heads):
        cols = slice(h * BLOCK, (h + 1) * BLOCK)
        coded[:, cols] = jnp.broadcast_to(codes[:, h : h + 1], (toks, BLOCK)).astype(BF16)
        coef[:, cols] = jnp.full((8, BLOCK), rate_ref[h] * (-12.288 / seq / 63.0), F32)
        skips[:, cols] = jnp.full((8, BLOCK), skip_ref[h], F32)

    pl.semaphore_wait(barrier, count)

    rims = [
        remote(x_hbm.at[pl.ds(toks - RIM, RIM)], rim_x, rim_send.at[0], rim_recv.at[0], ctx + 1, tp),
        remote(bc_ref.at[pl.ds(toks - RIM, RIM)], rim_bc, rim_send.at[1], rim_recv.at[1], ctx + 1, tp),
    ]

    @pl.when(ctx < n_ctx - 1)
    def _():
        for copy in rims:
            copy.start()

    chunks = owned // GROUP

    def w_load(r):
        first = pl.multiple_of(((iy + r) % n_y * 2 + core) * owned, GROUP)
        return pltpu.make_async_copy(w_ref.at[:, pl.ds(first, owned)], w_own.at[r], wl_sem.at[r])

    def w_swap(r, c):
        first = pl.multiple_of(((iy + r) % n_y * 2 + 1 - core) * owned + c * GROUP, GROUP)
        return remote(
            w_ref.at[:, pl.ds(first, GROUP)], w_sib.at[r, :, span_of(c)], ws_send.at[r, c], ws_recv.at[r, c], ctx, sib
        )

    def decays(j, _):
        cols = span_of(j)
        cum = jnp.dot(tril[...], coded[:, cols], preferred_element_type=F32) * coef[0:1, cols]
        ec[:, cols] = jnp.exp(cum)
        en[:, cols] = jnp.exp(-cum)
        return 0

    lax.fori_loop(0, groups, decays, 0)

    def conv_bc(b):
        rows = pl.ds(b * BLOCK, BLOCK)
        if b == 0:
            window = jnp.concatenate([rim_bc[...], bc_ref[rows, :]], axis=0)
        else:
            window = bc_ref[pl.ds(b * BLOCK - RIM, BLOCK + RIM), :]
        value = conv(window.astype(F32), cbc_ref[...], bbc_ref[...])
        bcc[rows, :] = value
        bt[:, b * BLOCK : (b + 1) * BLOCK] = value[:, :n_state].astype(F32).T.astype(BF16)

    for b in range(1, blocks):
        conv_bc(b)

    @pl.when(ctx == 0)
    def _():
        rim_x[...] = jnp.zeros_like(rim_x)
        rim_bc[...] = jnp.zeros_like(rim_bc)

    @pl.when(ctx > 0)
    def _():
        for copy in rims:
            copy.wait_recv()

    conv_bc(0)

    @pl.when(iz == 0)
    def _():
        pz[...] = jnp.zeros_like(pz)

    def strip_of(q):
        return pl.ds(pl.multiple_of(q * BLOCK, BLOCK), BLOCK)

    def x_copy(r, q):
        return remote(
            states.at[n_x - 1, :, strip_of(q)], states.at[r - 1, :, strip_of(q)],
            x_send.at[r - 1, q], x_recv.at[r - 1, q],
            iz * n_x + (ix + r) % n_x, tp,
        )

    def z_copy(q):
        return remote(pz_next.at[:, strip_of(q)], pz.at[:, strip_of(q)], z_send.at[q], z_recv.at[q], ctx + n_x, tp)

    def n_copy(g, b):
        rows = pl.ds(b * BLOCK, BLOCK)
        return remote(own_n.at[rows, span_of(g)], sib_n.at[rows, span_of(g)], n_send.at[g, b], n_recv.at[g, b], ctx, sib)

    def own_state(g):
        load_x(g).wait()
        for half in range(GROUP // BLOCK):
            cols = pl.ds(pl.multiple_of(g * GROUP + half * BLOCK, BLOCK), BLOCK)
            for b in range(blocks):
                rows = pl.ds(b * BLOCK, BLOCK)
                if b == 0:
                    window = jnp.concatenate([rim_x[:, cols], x_ref[rows, cols]], axis=0)
                else:
                    window = x_ref[pl.ds(b * BLOCK - RIM, BLOCK + RIM), cols]
                value = conv(window.astype(F32), cx_ref[:, cols], bx_ref[:, cols])
                xc[rows, cols] = value
                us[rows, cols] = (value.astype(F32) * en[rows, cols]).astype(BF16)
        cols = span_of(g)
        total = ec[toks - 1 : toks, cols]
        state = jnp.dot(bt[...], us[:, cols], preferred_element_type=F32)
        states[n_x - 1, :n_state, cols] = (state * total).astype(BF16)
        high = total.astype(BF16).astype(F32)
        pick = lax.broadcasted_iota(jnp.int32, (RIM, GROUP), 0) < 8
        states[n_x - 1, n_state:, cols] = jnp.where(pick, high, total - high).astype(BF16)
        for half in range(GROUP // BLOCK):
            for r in range(1, n_x):
                x_copy(r, g * (GROUP // BLOCK) + half).start()

    def score():
        load_z.wait()
        for b in range(blocks):
            rows = slice(b * BLOCK, (b + 1) * BLOCK)
            upto = (b + 1) * BLOCK
            scores = lax.dot_general(
                bcc[rows, n_state:], bcc[:upto, :n_state], (((1,), (1,)), ((), ())), preferred_element_type=F32
            )
            pm[rows, :upto] = (scores * tril[rows, :upto].astype(F32)).astype(BF16)

    scale = 1.0 / math.sqrt(n_state * seq)

    def inside(g):
        cols = span_of(g)
        for b in range(blocks):
            rows = slice(b * BLOCK, (b + 1) * BLOCK)
            upto = (b + 1) * BLOCK
            y = jnp.dot(pm[rows, :upto], us[:upto, cols], preferred_element_type=F32)
            gate = silu(z_ref[rows, cols].astype(F32))
            decay = ec[rows, cols] * (scale * gate)
            g_all[rows, cols] = y * decay + skips[0:1, cols] * xc[rows, cols].astype(F32) * gate
            h_all[rows, cols] = decay

    def prefix(g):
        for half in range(GROUP // BLOCK):
            q = g * (GROUP // BLOCK) + half
            cols = strip_of(q)
            for r in range(1, n_x):
                x_copy(r, q).wait_recv()
            pl.when(iz > 0)(functools.partial(lambda q: z_copy(q).wait_recv(), q))
            before = pz[:, cols].astype(F32)
            arrived = before
            for k in range(n_x):
                slot = (ix - k - 1 + n_x) % n_x
                arrived = jnp.where(ix == k, before, arrived)
                factor = states[slot, n_state : n_state + 1, cols].astype(F32)
                factor = factor + states[slot, n_state + 8 : n_state + 9, cols].astype(F32)
                before = before * factor + states[slot, :n_state, cols].astype(F32)
            pz_next[:, cols] = before.astype(BF16)
            pl.when(iz < n_z - 1)(functools.partial(lambda q: z_copy(q).start(), q))
            pin[:, cols] = arrived.astype(BF16)

    def norm(g):
        cols = span_of(g)
        for b in range(blocks):
            rows = slice(b * BLOCK, (b + 1) * BLOCK)
            carried = jnp.dot(bcc[rows, n_state:], pin[:, cols], preferred_element_type=F32)
            gated = g_all[rows, cols] + h_all[rows, cols] * carried
            for half in range(GROUP // BLOCK):
                piece = gated[:, half * BLOCK : (half + 1) * BLOCK]
                mean_square = jnp.mean(piece * piece, axis=-1, keepdims=True)
                cut = pl.ds(pl.multiple_of(g * GROUP + half * BLOCK, BLOCK), BLOCK)
                own_n[rows, cut] = (piece * lax.rsqrt(mean_square + 1e-05) * gain_ref[:, cut]).astype(BF16)
            n_copy(g, b).start()

    delay = jnp.where(iz == n_z - 1, 2 * groups, iz + 1)
    late = jnp.maximum(delay, groups)

    slots = groups + max(2 * groups, n_z)
    ahead = min(slots, (n_y - 1) * chunks)

    def first_loads():
        for r in range(1, n_y):
            w_load(r).start()

    def slot_step(s, _):
        pl.when(s < groups)(lambda: own_state(s))
        pl.when((s >= delay) & (s < delay + groups))(lambda: prefix(s - delay))
        pl.when(s < ahead)(lambda: w_swap(1 + s // chunks, s % chunks).start())
        pl.when(s == 1)(first_loads)
        pl.when(s == groups)(lambda: w_load(0).start())
        pl.when(s == groups)(score)
        pl.when((s >= groups) & (s < 2 * groups))(lambda: inside(s - groups))
        pl.when((s >= late) & (s < late + groups))(lambda: norm(s - late))
        return 0

    lax.fori_loop(0, slots, slot_step, 0)
    for k in range(ahead, (n_y - 1) * chunks):
        w_swap(1 + k // chunks, k % chunks).start()

    def project(b, r, first, tiles, store):
        rows = slice(b * BLOCK, (b + 1) * BLOCK)

        def tile(j, _):
            cols = pl.ds(pl.multiple_of(first + j * GROUP, GROUP), GROUP)
            value = jnp.dot(own_n[rows, :], w_own[r, :, cols], preferred_element_type=F32)
            value = value + jnp.dot(sib_n[rows, :], w_sib[r, :, cols], preferred_element_type=F32)
            store(rows, j, cols, value)
            return 0

        lax.fori_loop(0, tiles, tile, 0)

    y_copies = {}

    near = list(range(chunks))

    def send_block(b):
        for r in range(1, n_y):
            if b == 0:
                w_load(r).wait()
            for p in range(parts):
                if b == 0:
                    for c in range(p * part // GROUP, (p + 1) * part // GROUP):
                        w_swap(r, c).wait_recv()

                def store(rows, j, cols, value, r=r, p=p):
                    y_send[r - 1, p, rows, span_of(j)] = value.astype(BF16)

                project(b, r, p * part, part // GROUP, store)
                span = pl.ds(b * BLOCK, BLOCK)
                at = b * parts + p
                y_copies[b, r, p] = remote(
                    y_send.at[r - 1, p, span], y_recv.at[r - 1, p, span],
                    ys_send.at[r - 1, at], ys_recv.at[r - 1, at],
                    ctx, (iy + r) % n_y * 2 + core,
                )
                y_copies[b, r, p].start()
                if near:
                    w_swap(0, near.pop(0)).start()

    for b in range(blocks):
        for g in range(groups):
            n_copy(g, b).wait_recv()
        send_block(b)

    for c in near:
        w_swap(0, c).start()
    w_load(0).wait()
    for c in range(chunks):
        w_swap(0, c).wait_recv()

    def keep(rows, j, cols, value):
        local[rows, cols] = value

    for b in range(blocks):
        project(b, 0, 0, owned // GROUP, keep)

    for b in range(blocks):
        rows = slice(b * BLOCK, (b + 1) * BLOCK)
        for p in range(parts):
            cols = slice(p * part, (p + 1) * part)
            total = local[rows, cols]
            for r in range(1, n_y):
                y_copies[b, r, p].wait_recv()
                total = total + y_recv[r - 1, p, rows, :].astype(F32)
            out_ref[rows, cols] = total.astype(BF16)

    @pl.when(ctx < n_ctx - 1)
    def _():
        for copy in rims:
            copy.wait_send()

    @pl.when(iz < n_z - 1)
    def _():
        for q in range(width // BLOCK):
            z_copy(q).wait_send()

    for g in range(groups):
        for b in range(blocks):
            n_copy(g, b).wait_send()
    for q in range(width // BLOCK):
        for r in range(1, n_x):
            x_copy(r, q).wait_send()
    for r in range(n_y):
        for c in range(chunks):
            w_swap(r, c).wait_send()
    for copy in y_copies.values():
        copy.wait_send()


def solution(mesh):
    n_ctx, n_tp = mesh.shape["ctx"], mesh.shape["tp"]
    n_x = max(1, n_ctx // 4)

    def body(x_in, bc_in, z_in, codes, head_rate, conv_x, conv_bc, bias_x, bias_bc, skip, norm_gain, w_out):
        toks, width = x_in.shape
        maps = bc_in.shape[1]
        n_state = maps // 2
        depth, model = w_out.shape
        owned = model // n_tp
        part = min(owned, 512)
        n_y = n_tp // 2
        far = max(1, n_y - 1)
        row = max(1, n_x - 1)
        groups = width // GROUP
        strips = width // BLOCK
        blocks = toks // BLOCK
        vmem = pl.BlockSpec(memory_space=pltpu.VMEM)
        hbm = pl.BlockSpec(memory_space=pl.ANY)
        smem = pl.BlockSpec(memory_space=pltpu.SMEM)
        dma = pltpu.SemaphoreType.DMA
        pieces = blocks * (owned // part)
        return pl.pallas_call(
            functools.partial(layer, n_ctx, n_tp, n_x),
            out_shape=pltpu.VMEM((toks, owned), BF16),
            in_specs=[hbm, vmem, hbm, vmem, smem, vmem, vmem, vmem, vmem, smem, vmem, hbm],
            out_specs=vmem,
            scratch_shapes=[
                pltpu.VMEM((toks, width), BF16),
                pltpu.VMEM((toks, width), BF16),
                pltpu.VMEM((toks, toks), BF16),
                pltpu.VMEM((RIM, width), BF16),
                pltpu.VMEM((RIM, maps), BF16),
                pltpu.VMEM((toks, toks), BF16),
                pltpu.VMEM((toks, width), BF16),
                pltpu.VMEM((8, width), F32),
                pltpu.VMEM((8, width), F32),
                pltpu.VMEM((toks, width), F32),
                pltpu.VMEM((toks, width), F32),
                pltpu.VMEM((toks, maps), BF16),
                pltpu.VMEM((n_state, toks), BF16),
                pltpu.VMEM((toks, width), BF16),
                pltpu.VMEM((toks, width), BF16),
                pltpu.VMEM((n_x, n_state + RIM, width), BF16),
                pltpu.VMEM((n_state, width), BF16),
                pltpu.VMEM((n_state, width), BF16),
                pltpu.VMEM((n_state, width), BF16),
                pltpu.VMEM((toks, width), F32),
                pltpu.VMEM((toks, width), F32),
                pltpu.VMEM((toks, width), BF16),
                pltpu.VMEM((toks, width), BF16),
                pltpu.VMEM((n_y, depth, owned), BF16),
                pltpu.VMEM((n_y, depth, owned), BF16),
                pltpu.VMEM((far, owned // part, toks, part), BF16),
                pltpu.VMEM((far, owned // part, toks, part), BF16),
                pltpu.VMEM((toks, owned), F32),
                dma((groups,)), dma((1,)), dma((2,)), dma((2,)),
                dma((n_y,)), dma((n_y, owned // GROUP)), dma((n_y, owned // GROUP)),
                dma((row, strips)), dma((row, strips)),
                dma((strips,)), dma((strips,)),
                dma((groups, blocks)), dma((groups, blocks)),
                dma((far, pieces)), dma((far, pieces)),
            ],
            compiler_params=pltpu.CompilerParams(
                collective_id=0, has_side_effects=True, vmem_limit_bytes=58 * 1024 * 1024
            ),
        )(x_in, bc_in, z_in, codes.T, head_rate, conv_x, conv_bc, bias_x[None], bias_bc[None], skip,
          norm_gain[None], w_out)

    in_specs = (
        P("ctx", "tp"), P("ctx", None), P("ctx", "tp"), P("ctx", "tp"), P("tp"), P(None, "tp"),
        P(), P("tp"), P(), P("tp"), P("tp"), P("tp", None),
    )
    return jax.shard_map(body, mesh=mesh, in_specs=in_specs, out_specs=P("ctx", "tp"), check_vma=False)
```

```python
import functools
import math

import jax
import jax.numpy as jnp
from jax import lax
from jax.experimental import pallas as pl
from jax.experimental.pallas import tpu as pltpu
from jax.sharding import PartitionSpec as P

MESH = pl.DeviceIdType.MESH
F32 = jnp.float32
BF16 = jnp.bfloat16
BLOCK = 128
GROUP = 256
RIM = 16


def silu(v):
    half = 0.5 * v
    return half + half * jnp.tanh(half)


def conv(window, taps, bias):
    total = bias + taps[3:4] * window[RIM:]
    for k in range(3):
        total = total + taps[k : k + 1] * pltpu.roll(window, 3 - k, 0)[RIM:]
    return silu(total).astype(BF16)


def layer(
    n_ctx,
    n_tp,
    n_x,
    x_hbm, bc_ref, z_hbm, codes_ref, rate_ref, cx_ref, cbc_ref, bx_ref, bbc_ref, skip_ref, gain_ref, w_ref,
    out_ref,
    x_ref, z_ref, pm, rim_x, rim_bc, tril, coded, coef, skips, cum, bcc, bt, xc, us, states, pz, pz_next, pin,
    g_all, h_all, own_n, sib_n, w_own, w_sib, y_send, y_recv, local,
    xl_sem, zl_sem, rim_send, rim_recv, wl_sem, ws_send, ws_recv, x_send, x_recv, z_send, z_recv, n_send, n_recv, ys_send, ys_recv,
):
    toks, width = x_hbm.shape
    heads = skip_ref.shape[0]
    n_z = n_ctx // n_x
    n_y = n_tp // 2
    blocks = toks // BLOCK
    groups = width // GROUP
    owned = out_ref.shape[1]
    part = y_send.shape[3]
    parts = owned // part
    ctx = lax.axis_index("ctx")
    tp = lax.axis_index("tp")
    iz, ix = ctx // n_x, ctx % n_x
    iy, core = tp // 2, tp % 2
    sib = tp + 1 - 2 * core
    seq = toks * n_ctx
    n_state = bc_ref.shape[1] // 2

    barrier = pltpu.get_barrier_semaphore()

    def greet(c, t):
        pl.semaphore_signal(barrier, inc=1, device_id=(c, t), device_id_type=MESH)

    greet(ctx, sib)
    for r in range(1, n_y):
        greet(ctx, (iy + r) % n_y * 2 + core)
    for r in range(1, n_x):
        greet(iz * n_x + (ix + r) % n_x, tp)
    for near, far in ((ctx > 0, ctx - 1), (ctx < n_ctx - 1, ctx + 1), (iz > 0, ctx - n_x), (iz < n_z - 1, ctx + n_x)):
        pl.when(near)(functools.partial(greet, far, tp))
    count = n_y + n_x - 1
    for near in (ctx > 0, ctx < n_ctx - 1, iz > 0, iz < n_z - 1):
        count = count + jnp.where(near, 1, 0)

    def remote(src, dst, send, recv, c, t):
        return pltpu.make_async_remote_copy(
            src_ref=src, dst_ref=dst, send_sem=send, recv_sem=recv, device_id=(c, t), device_id_type=MESH
        )

    def span_of(g):
        return pl.ds(pl.multiple_of(g * GROUP, GROUP), GROUP)

    def load_x(g):
        return pltpu.make_async_copy(x_hbm.at[:, span_of(g)], x_ref.at[:, span_of(g)], xl_sem.at[g])

    load_z = pltpu.make_async_copy(z_hbm, z_ref, zl_sem.at[0])
    for g in range(groups):
        load_x(g).start()
    load_z.start()

    row_id = lax.broadcasted_iota(jnp.int32, (toks, toks), 0)
    col_id = lax.broadcasted_iota(jnp.int32, (toks, toks), 1)
    tril[...] = jnp.where(row_id >= col_id, 1.0, 0.0).astype(BF16)
    codes = codes_ref[...].astype(F32).T
    for h in range(heads):
        cols = slice(h * BLOCK, (h + 1) * BLOCK)
        coded[:, cols] = jnp.broadcast_to(codes[:, h : h + 1], (toks, BLOCK)).astype(BF16)
        coef[:, cols] = jnp.full((8, BLOCK), rate_ref[h] * (-12.288 / seq / 63.0), F32)
        skips[:, cols] = jnp.full((8, BLOCK), skip_ref[h], F32)

    pl.semaphore_wait(barrier, count)

    rims = [
        remote(x_hbm.at[pl.ds(toks - RIM, RIM)], rim_x, rim_send.at[0], rim_recv.at[0], ctx + 1, tp),
        remote(bc_ref.at[pl.ds(toks - RIM, RIM)], rim_bc, rim_send.at[1], rim_recv.at[1], ctx + 1, tp),
    ]

    @pl.when(ctx < n_ctx - 1)
    def _():
        for copy in rims:
            copy.start()

    chunks = owned // GROUP

    def w_load(r):
        first = pl.multiple_of(((iy + r) % n_y * 2 + core) * owned, GROUP)
        return pltpu.make_async_copy(w_ref.at[:, pl.ds(first, owned)], w_own.at[r], wl_sem.at[r])

    def w_swap(r, c):
        first = pl.multiple_of(((iy + r) % n_y * 2 + 1 - core) * owned + c * GROUP, GROUP)
        return remote(
            w_ref.at[:, pl.ds(first, GROUP)], w_sib.at[r, :, span_of(c)], ws_send.at[r, c], ws_recv.at[r, c], ctx, sib
        )

    def decays(j, _):
        cols = span_of(j)
        cum[:, cols] = jnp.dot(tril[...], coded[:, cols], preferred_element_type=F32) * coef[0:1, cols]
        return 0

    lax.fori_loop(0, groups, decays, 0)

    def conv_bc(b):
        rows = pl.ds(b * BLOCK, BLOCK)
        if b == 0:
            window = jnp.concatenate([rim_bc[...], bc_ref[rows, :]], axis=0)
        else:
            window = bc_ref[pl.ds(b * BLOCK - RIM, BLOCK + RIM), :]
        value = conv(window.astype(F32), cbc_ref[...], bbc_ref[...])
        bcc[rows, :] = value
        bt[:, b * BLOCK : (b + 1) * BLOCK] = value[:, :n_state].astype(F32).T.astype(BF16)

    for b in range(1, blocks):
        conv_bc(b)

    @pl.when(ctx == 0)
    def _():
        rim_x[...] = jnp.zeros_like(rim_x)
        rim_bc[...] = jnp.zeros_like(rim_bc)

    @pl.when(ctx > 0)
    def _():
        for copy in rims:
            copy.wait_recv()

    conv_bc(0)

    @pl.when(iz == 0)
    def _():
        pz[...] = jnp.zeros_like(pz)

    def strip_of(q):
        return pl.ds(pl.multiple_of(q * BLOCK, BLOCK), BLOCK)

    def x_copy(r, q):
        return remote(
            states.at[n_x - 1, :, strip_of(q)], states.at[r - 1, :, strip_of(q)],
            x_send.at[r - 1, q], x_recv.at[r - 1, q],
            iz * n_x + (ix + r) % n_x, tp,
        )

    def z_copy(q):
        return remote(pz_next.at[:, strip_of(q)], pz.at[:, strip_of(q)], z_send.at[q], z_recv.at[q], ctx + n_x, tp)

    def n_copy(g, b):
        rows = pl.ds(b * BLOCK, BLOCK)
        return remote(own_n.at[rows, span_of(g)], sib_n.at[rows, span_of(g)], n_send.at[g, b], n_recv.at[g, b], ctx, sib)

    def own_state(g):
        load_x(g).wait()
        for half in range(GROUP // BLOCK):
            cols = pl.ds(pl.multiple_of(g * GROUP + half * BLOCK, BLOCK), BLOCK)
            for b in range(blocks):
                rows = pl.ds(b * BLOCK, BLOCK)
                if b == 0:
                    window = jnp.concatenate([rim_x[:, cols], x_ref[rows, cols]], axis=0)
                else:
                    window = x_ref[pl.ds(b * BLOCK - RIM, BLOCK + RIM), cols]
                value = conv(window.astype(F32), cx_ref[:, cols], bx_ref[:, cols])
                xc[rows, cols] = value
                us[rows, cols] = (value.astype(F32) * jnp.exp(-cum[rows, cols])).astype(BF16)
        cols = span_of(g)
        total = jnp.exp(cum[toks - 1 : toks, cols])
        state = jnp.dot(bt[...], us[:, cols], preferred_element_type=F32)
        states[n_x - 1, :n_state, cols] = (state * total).astype(BF16)
        high = total.astype(BF16).astype(F32)
        pick = lax.broadcasted_iota(jnp.int32, (RIM, GROUP), 0) < 8
        states[n_x - 1, n_state:, cols] = jnp.where(pick, high, total - high).astype(BF16)
        for half in range(GROUP // BLOCK):
            for r in range(1, n_x):
                x_copy(r, g * (GROUP // BLOCK) + half).start()

    def score():
        load_z.wait()
        for b in range(blocks):
            rows = slice(b * BLOCK, (b + 1) * BLOCK)
            upto = (b + 1) * BLOCK
            scores = lax.dot_general(
                bcc[rows, n_state:], bcc[:upto, :n_state], (((1,), (1,)), ((), ())), preferred_element_type=F32
            )
            pm[rows, :upto] = (scores * tril[rows, :upto].astype(F32)).astype(BF16)

    scale = 1.0 / math.sqrt(n_state * seq)

    def inside(g):
        cols = span_of(g)
        for b in range(blocks):
            rows = slice(b * BLOCK, (b + 1) * BLOCK)
            upto = (b + 1) * BLOCK
            y = jnp.dot(pm[rows, :upto], us[:upto, cols], preferred_element_type=F32)
            gate = silu(z_ref[rows, cols].astype(F32))
            decay = jnp.exp(cum[rows, cols]) * (scale * gate)
            g_all[rows, cols] = y * decay + skips[0:1, cols] * xc[rows, cols].astype(F32) * gate
            h_all[rows, cols] = decay

    def prefix(g):
        for half in range(GROUP // BLOCK):
            q = g * (GROUP // BLOCK) + half
            cols = strip_of(q)
            for r in range(1, n_x):
                x_copy(r, q).wait_recv()
            pl.when(iz > 0)(functools.partial(lambda q: z_copy(q).wait_recv(), q))
            before = pz[:, cols].astype(F32)
            arrived = before
            for k in range(n_x):
                slot = (ix - k - 1 + n_x) % n_x
                arrived = jnp.where(ix == k, before, arrived)
                factor = states[slot, n_state : n_state + 1, cols].astype(F32)
                factor = factor + states[slot, n_state + 8 : n_state + 9, cols].astype(F32)
                before = before * factor + states[slot, :n_state, cols].astype(F32)
            pz_next[:, cols] = before.astype(BF16)
            pl.when(iz < n_z - 1)(functools.partial(lambda q: z_copy(q).start(), q))
            pin[:, cols] = arrived.astype(BF16)

    def norm(g):
        cols = span_of(g)
        for b in range(blocks):
            rows = slice(b * BLOCK, (b + 1) * BLOCK)
            carried = jnp.dot(bcc[rows, n_state:], pin[:, cols], preferred_element_type=F32)
            gated = g_all[rows, cols] + h_all[rows, cols] * carried
            for half in range(GROUP // BLOCK):
                piece = gated[:, half * BLOCK : (half + 1) * BLOCK]
                mean_square = jnp.mean(piece * piece, axis=-1, keepdims=True)
                cut = pl.ds(pl.multiple_of(g * GROUP + half * BLOCK, BLOCK), BLOCK)
                own_n[rows, cut] = (piece * lax.rsqrt(mean_square + 1e-05) * gain_ref[:, cut]).astype(BF16)
            n_copy(g, b).start()

    delay = jnp.where(iz == n_z - 1, 2 * groups, iz + 1)
    late = jnp.maximum(delay, groups)

    slots = groups + max(2 * groups, n_z)
    ahead = min(slots, (n_y - 1) * chunks)

    def first_loads():
        for r in range(1, n_y):
            w_load(r).start()

    def slot_step(s, _):
        pl.when(s < groups)(lambda: own_state(s))
        pl.when((s >= delay) & (s < delay + groups))(lambda: prefix(s - delay))
        pl.when(s < ahead)(lambda: w_swap(1 + s // chunks, s % chunks).start())
        pl.when(s == 1)(first_loads)
        pl.when(s == groups)(lambda: w_load(0).start())
        pl.when(s == groups)(score)
        pl.when((s >= groups) & (s < 2 * groups))(lambda: inside(s - groups))
        pl.when((s >= late) & (s < late + groups))(lambda: norm(s - late))
        return 0

    lax.fori_loop(0, slots, slot_step, 0)
    for k in range(ahead, (n_y - 1) * chunks):
        w_swap(1 + k // chunks, k % chunks).start()

    def project(rows, r, first, tiles, store):

        def tile(j, _):
            cols = pl.ds(pl.multiple_of(first + j * GROUP, GROUP), GROUP)
            value = jnp.dot(own_n[rows, :], w_own[r, :, cols], preferred_element_type=F32)
            value = value + jnp.dot(sib_n[rows, :], w_sib[r, :, cols], preferred_element_type=F32)
            store(rows, j, cols, value)
            return 0

        lax.fori_loop(0, tiles, tile, 0)

    y_copies = {}

    near = list(range(chunks))

    def send_rows(k, low, high):
        rows = slice(low, high)
        for r in range(1, n_y):
            if k == 0:
                w_load(r).wait()
            for p in range(parts):
                if k == 0:
                    for c in range(p * part // GROUP, (p + 1) * part // GROUP):
                        w_swap(r, c).wait_recv()

                def store(rows, j, cols, value, r=r, p=p):
                    y_send[r - 1, p, rows, span_of(j)] = value.astype(BF16)

                project(rows, r, p * part, part // GROUP, store)
                span = pl.ds(low, high - low)
                at = k * parts + p
                y_copies[k, r, p] = remote(
                    y_send.at[r - 1, p, span], y_recv.at[r - 1, p, span],
                    ys_send.at[r - 1, at], ys_recv.at[r - 1, at],
                    ctx, (iy + r) % n_y * 2 + core,
                )
                y_copies[k, r, p].start()
                if near:
                    w_swap(0, near.pop(0)).start()

    stretches = [(0, BLOCK), (BLOCK, toks)]
    for k, (low, high) in enumerate(stretches):
        for b in range(low // BLOCK, high // BLOCK):
            for g in range(groups):
                n_copy(g, b).wait_recv()
        send_rows(k, low, high)

    for c in near:
        w_swap(0, c).start()
    w_load(0).wait()
    for c in range(chunks):
        w_swap(0, c).wait_recv()

    def keep(rows, j, cols, value):
        local[rows, cols] = value

    project(slice(0, toks), 0, 0, chunks, keep)

    for k, (low, high) in enumerate(stretches):
        rows = slice(low, high)
        for p in range(parts):
            cols = slice(p * part, (p + 1) * part)
            total = local[rows, cols]
            for r in range(1, n_y):
                y_copies[k, r, p].wait_recv()
                total = total + y_recv[r - 1, p, rows, :].astype(F32)
            out_ref[rows, cols] = total.astype(BF16)

    @pl.when(ctx < n_ctx - 1)
    def _():
        for copy in rims:
            copy.wait_send()

    @pl.when(iz < n_z - 1)
    def _():
        for q in range(width // BLOCK):
            z_copy(q).wait_send()

    for g in range(groups):
        for b in range(blocks):
            n_copy(g, b).wait_send()
    for q in range(width // BLOCK):
        for r in range(1, n_x):
            x_copy(r, q).wait_send()
    for r in range(n_y):
        for c in range(chunks):
            w_swap(r, c).wait_send()
    for copy in y_copies.values():
        copy.wait_send()


def solution(mesh):
    n_ctx, n_tp = mesh.shape["ctx"], mesh.shape["tp"]
    n_x = max(1, n_ctx // 4)

    def body(x_in, bc_in, z_in, codes, head_rate, conv_x, conv_bc, bias_x, bias_bc, skip, norm_gain, w_out):
        toks, width = x_in.shape
        maps = bc_in.shape[1]
        n_state = maps // 2
        depth, model = w_out.shape
        owned = model // n_tp
        part = min(owned, 512)
        n_y = n_tp // 2
        far = max(1, n_y - 1)
        row = max(1, n_x - 1)
        groups = width // GROUP
        strips = width // BLOCK
        blocks = toks // BLOCK
        vmem = pl.BlockSpec(memory_space=pltpu.VMEM)
        hbm = pl.BlockSpec(memory_space=pl.ANY)
        smem = pl.BlockSpec(memory_space=pltpu.SMEM)
        dma = pltpu.SemaphoreType.DMA
        pieces = 2 * (owned // part)
        return pl.pallas_call(
            functools.partial(layer, n_ctx, n_tp, n_x),
            out_shape=pltpu.VMEM((toks, owned), BF16),
            in_specs=[hbm, vmem, hbm, vmem, smem, vmem, vmem, vmem, vmem, smem, vmem, hbm],
            out_specs=vmem,
            scratch_shapes=[
                pltpu.VMEM((toks, width), BF16),
                pltpu.VMEM((toks, width), BF16),
                pltpu.VMEM((toks, toks), BF16),
                pltpu.VMEM((RIM, width), BF16),
                pltpu.VMEM((RIM, maps), BF16),
                pltpu.VMEM((toks, toks), BF16),
                pltpu.VMEM((toks, width), BF16),
                pltpu.VMEM((8, width), F32),
                pltpu.VMEM((8, width), F32),
                pltpu.VMEM((toks, width), F32),
                pltpu.VMEM((toks, maps), BF16),
                pltpu.VMEM((n_state, toks), BF16),
                pltpu.VMEM((toks, width), BF16),
                pltpu.VMEM((toks, width), BF16),
                pltpu.VMEM((n_x, n_state + RIM, width), BF16),
                pltpu.VMEM((n_state, width), BF16),
                pltpu.VMEM((n_state, width), BF16),
                pltpu.VMEM((n_state, width), BF16),
                pltpu.VMEM((toks, width), F32),
                pltpu.VMEM((toks, width), F32),
                pltpu.VMEM((toks, width), BF16),
                pltpu.VMEM((toks, width), BF16),
                pltpu.VMEM((n_y, depth, owned), BF16),
                pltpu.VMEM((n_y, depth, owned), BF16),
                pltpu.VMEM((far, owned // part, toks, part), BF16),
                pltpu.VMEM((far, owned // part, toks, part), BF16),
                pltpu.VMEM((toks, owned), F32),
                dma((groups,)), dma((1,)), dma((2,)), dma((2,)),
                dma((n_y,)), dma((n_y, owned // GROUP)), dma((n_y, owned // GROUP)),
                dma((row, strips)), dma((row, strips)),
                dma((strips,)), dma((strips,)),
                dma((groups, blocks)), dma((groups, blocks)),
                dma((far, pieces)), dma((far, pieces)),
            ],
            compiler_params=pltpu.CompilerParams(
                collective_id=0, has_side_effects=True, vmem_limit_bytes=58 * 1024 * 1024
            ),
        )(x_in, bc_in, z_in, codes.T, head_rate, conv_x, conv_bc, bias_x[None], bias_bc[None], skip,
          norm_gain[None], w_out)

    in_specs = (
        P("ctx", "tp"), P("ctx", None), P("ctx", "tp"), P("ctx", "tp"), P("tp"), P(None, "tp"),
        P(), P("tp"), P(), P("tp"), P("tp"), P("tp", None),
    )
    return jax.shard_map(body, mesh=mesh, in_specs=in_specs, out_specs=P("ctx", "tp"), check_vma=False)
```

```python
import functools
import math

import jax
import jax.numpy as jnp
from jax import lax
from jax.experimental import pallas as pl
from jax.experimental.pallas import tpu as pltpu
from jax.sharding import PartitionSpec as P

MESH = pl.DeviceIdType.MESH
F32 = jnp.float32
BF16 = jnp.bfloat16
BLOCK = 128
GROUP = 256
RIM = 16


def silu(v):
    half = 0.5 * v
    return half + half * jnp.tanh(half)


def conv(window, taps, bias):
    total = bias + taps[3:4] * window[RIM:]
    for k in range(3):
        total = total + taps[k : k + 1] * pltpu.roll(window, 3 - k, 0)[RIM:]
    return silu(total).astype(BF16)


def layer(
    n_ctx,
    n_tp,
    n_x,
    x_hbm, bc_ref, z_hbm, codes_ref, rate_ref, cx_ref, cbc_ref, bx_ref, bbc_ref, skip_ref, gain_ref, w_ref,
    out_ref,
    x_ref, z_ref, pm, rim_x, rim_bc, tril, coded, coef, skips, cum, bcc, bt, xc, us, states, pz, pz_next, pin,
    g_all, h_all, own_n, sib_n, w_own, w_sib, y_send, y_recv, local,
    xl_sem, zl_sem, rim_send, rim_recv, wl_sem, ws_send, ws_recv, x_send, x_recv, z_send, z_recv, n_send, n_recv, ys_send, ys_recv,
):
    toks, width = x_hbm.shape
    heads = skip_ref.shape[0]
    n_z = n_ctx // n_x
    n_y = n_tp // 2
    blocks = toks // BLOCK
    groups = width // GROUP
    owned = out_ref.shape[1]
    part = y_send.shape[3]
    parts = owned // part
    ctx = lax.axis_index("ctx")
    tp = lax.axis_index("tp")
    iz, ix = ctx // n_x, ctx % n_x
    iy, core = tp // 2, tp % 2
    sib = tp + 1 - 2 * core
    seq = toks * n_ctx
    n_state = bc_ref.shape[1] // 2

    barrier = pltpu.get_barrier_semaphore()

    def greet(c, t):
        pl.semaphore_signal(barrier, inc=1, device_id=(c, t), device_id_type=MESH)

    greet(ctx, sib)
    for r in range(1, n_y):
        greet(ctx, (iy + r) % n_y * 2 + core)
    for r in range(1, n_x):
        greet(iz * n_x + (ix + r) % n_x, tp)
    for near, far in ((ctx > 0, ctx - 1), (ctx < n_ctx - 1, ctx + 1), (iz > 0, ctx - n_x), (iz < n_z - 1, ctx + n_x)):
        pl.when(near)(functools.partial(greet, far, tp))
    count = n_y + n_x - 1
    for near in (ctx > 0, ctx < n_ctx - 1, iz > 0, iz < n_z - 1):
        count = count + jnp.where(near, 1, 0)

    def remote(src, dst, send, recv, c, t):
        return pltpu.make_async_remote_copy(
            src_ref=src, dst_ref=dst, send_sem=send, recv_sem=recv, device_id=(c, t), device_id_type=MESH
        )

    def span_of(g):
        return pl.ds(pl.multiple_of(g * GROUP, GROUP), GROUP)

    def load_x(g):
        return pltpu.make_async_copy(x_hbm.at[:, span_of(g)], x_ref.at[:, span_of(g)], xl_sem.at[g])

    load_z = pltpu.make_async_copy(z_hbm, z_ref, zl_sem.at[0])
    for g in range(groups):
        load_x(g).start()
    load_z.start()

    row_id = lax.broadcasted_iota(jnp.int32, (toks, toks), 0)
    col_id = lax.broadcasted_iota(jnp.int32, (toks, toks), 1)
    tril[...] = jnp.where(row_id >= col_id, 1.0, 0.0).astype(BF16)
    codes = codes_ref[...].astype(F32).T
    for h in range(heads):
        cols = slice(h * BLOCK, (h + 1) * BLOCK)
        coded[:, cols] = jnp.broadcast_to(codes[:, h : h + 1], (toks, BLOCK)).astype(BF16)
        coef[:, cols] = jnp.full((8, BLOCK), rate_ref[h] * (-12.288 / seq / 63.0), F32)
        skips[:, cols] = jnp.full((8, BLOCK), skip_ref[h], F32)

    pl.semaphore_wait(barrier, count)

    rims = [
        remote(x_hbm.at[pl.ds(toks - RIM, RIM)], rim_x, rim_send.at[0], rim_recv.at[0], ctx + 1, tp),
        remote(bc_ref.at[pl.ds(toks - RIM, RIM)], rim_bc, rim_send.at[1], rim_recv.at[1], ctx + 1, tp),
    ]

    @pl.when(ctx < n_ctx - 1)
    def _():
        for copy in rims:
            copy.start()

    chunks = owned // GROUP

    def w_load(r):
        first = pl.multiple_of(((iy + r) % n_y * 2 + core) * owned, GROUP)
        return pltpu.make_async_copy(w_ref.at[:, pl.ds(first, owned)], w_own.at[r], wl_sem.at[r])

    def w_swap(r, c):
        first = pl.multiple_of(((iy + r) % n_y * 2 + 1 - core) * owned + c * GROUP, GROUP)
        return remote(
            w_ref.at[:, pl.ds(first, GROUP)], w_sib.at[r, :, span_of(c)], ws_send.at[r, c], ws_recv.at[r, c], ctx, sib
        )

    def decays(j, _):
        cols = span_of(j)
        cum[:, cols] = jnp.dot(tril[...], coded[:, cols], preferred_element_type=F32) * coef[0:1, cols]
        return 0

    lax.fori_loop(0, groups, decays, 0)

    def conv_bc(b):
        rows = pl.ds(b * BLOCK, BLOCK)
        if b == 0:
            window = jnp.concatenate([rim_bc[...], bc_ref[rows, :]], axis=0)
        else:
            window = bc_ref[pl.ds(b * BLOCK - RIM, BLOCK + RIM), :]
        value = conv(window.astype(F32), cbc_ref[...], bbc_ref[...])
        bcc[rows, :] = value
        bt[:, b * BLOCK : (b + 1) * BLOCK] = value[:, :n_state].astype(F32).T.astype(BF16)

    for b in range(1, blocks):
        conv_bc(b)

    @pl.when(ctx == 0)
    def _():
        rim_x[...] = jnp.zeros_like(rim_x)
        rim_bc[...] = jnp.zeros_like(rim_bc)

    @pl.when(ctx > 0)
    def _():
        for copy in rims:
            copy.wait_recv()

    conv_bc(0)

    @pl.when(iz == 0)
    def _():
        pz[...] = jnp.zeros_like(pz)

    def strip_of(q):
        return pl.ds(pl.multiple_of(q * BLOCK, BLOCK), BLOCK)

    def x_copy(r, q):
        return remote(
            states.at[n_x - 1, :, strip_of(q)], states.at[r - 1, :, strip_of(q)],
            x_send.at[r - 1, q], x_recv.at[r - 1, q],
            iz * n_x + (ix + r) % n_x, tp,
        )

    def z_copy(q):
        return remote(pz_next.at[:, strip_of(q)], pz.at[:, strip_of(q)], z_send.at[q], z_recv.at[q], ctx + n_x, tp)

    def n_copy(g, b):
        rows = pl.ds(b * BLOCK, BLOCK)
        return remote(own_n.at[rows, span_of(g)], sib_n.at[rows, span_of(g)], n_send.at[g, b], n_recv.at[g, b], ctx, sib)

    def own_state(g):
        load_x(g).wait()
        for half in range(GROUP // BLOCK):
            cols = pl.ds(pl.multiple_of(g * GROUP + half * BLOCK, BLOCK), BLOCK)
            for b in range(blocks):
                rows = pl.ds(b * BLOCK, BLOCK)
                if b == 0:
                    window = jnp.concatenate([rim_x[:, cols], x_ref[rows, cols]], axis=0)
                else:
                    window = x_ref[pl.ds(b * BLOCK - RIM, BLOCK + RIM), cols]
                value = conv(window.astype(F32), cx_ref[:, cols], bx_ref[:, cols])
                xc[rows, cols] = value
                us[rows, cols] = (value.astype(F32) * jnp.exp(-cum[rows, cols])).astype(BF16)
        cols = span_of(g)
        total = jnp.exp(cum[toks - 1 : toks, cols])
        state = jnp.dot(bt[...], us[:, cols], preferred_element_type=F32)
        states[n_x - 1, :n_state, cols] = (state * total).astype(BF16)
        high = total.astype(BF16).astype(F32)
        pick = lax.broadcasted_iota(jnp.int32, (RIM, GROUP), 0) < 8
        states[n_x - 1, n_state:, cols] = jnp.where(pick, high, total - high).astype(BF16)
        for half in range(GROUP // BLOCK):
            for r in range(1, n_x):
                x_copy(r, g * (GROUP // BLOCK) + half).start()

    def score():
        load_z.wait()
        for b in range(blocks):
            rows = slice(b * BLOCK, (b + 1) * BLOCK)
            upto = (b + 1) * BLOCK
            scores = lax.dot_general(
                bcc[rows, n_state:], bcc[:upto, :n_state], (((1,), (1,)), ((), ())), preferred_element_type=F32
            )
            pm[rows, :upto] = (scores * tril[rows, :upto].astype(F32)).astype(BF16)

    scale = 1.0 / math.sqrt(n_state * seq)

    def inside(g, some):
        cols = span_of(g)
        for b in some:
            rows = slice(b * BLOCK, (b + 1) * BLOCK)
            upto = (b + 1) * BLOCK
            y = jnp.dot(pm[rows, :upto], us[:upto, cols], preferred_element_type=F32)
            gate = silu(z_ref[rows, cols].astype(F32))
            decay = jnp.exp(cum[rows, cols]) * (scale * gate)
            g_all[rows, cols] = y * decay + skips[0:1, cols] * xc[rows, cols].astype(F32) * gate
            h_all[rows, cols] = decay

    def prefix(g):
        for half in range(GROUP // BLOCK):
            q = g * (GROUP // BLOCK) + half
            cols = strip_of(q)
            for r in range(1, n_x):
                x_copy(r, q).wait_recv()
            pl.when(iz > 0)(functools.partial(lambda q: z_copy(q).wait_recv(), q))
            before = pz[:, cols].astype(F32)
            arrived = before
            for k in range(n_x):
                slot = (ix - k - 1 + n_x) % n_x
                arrived = jnp.where(ix == k, before, arrived)
                factor = states[slot, n_state : n_state + 1, cols].astype(F32)
                factor = factor + states[slot, n_state + 8 : n_state + 9, cols].astype(F32)
                before = before * factor + states[slot, :n_state, cols].astype(F32)
            pz_next[:, cols] = before.astype(BF16)
            pl.when(iz < n_z - 1)(functools.partial(lambda q: z_copy(q).start(), q))
            pin[:, cols] = arrived.astype(BF16)

    def norm(g, some):
        cols = span_of(g)
        for b in some:
            rows = slice(b * BLOCK, (b + 1) * BLOCK)
            carried = jnp.dot(bcc[rows, n_state:], pin[:, cols], preferred_element_type=F32)
            gated = g_all[rows, cols] + h_all[rows, cols] * carried
            for half in range(GROUP // BLOCK):
                piece = gated[:, half * BLOCK : (half + 1) * BLOCK]
                mean_square = jnp.mean(piece * piece, axis=-1, keepdims=True)
                cut = pl.ds(pl.multiple_of(g * GROUP + half * BLOCK, BLOCK), BLOCK)
                own_n[rows, cut] = (piece * lax.rsqrt(mean_square + 1e-05) * gain_ref[:, cut]).astype(BF16)
            n_copy(g, b).start()

    delay = jnp.where(iz == n_z - 1, 2 * groups, iz + 1)
    late = jnp.maximum(delay, groups)

    slots = groups + max(2 * groups, n_z)
    ahead = min(slots, (n_y - 1) * chunks)

    def first_loads():
        for r in range(1, n_y):
            w_load(r).start()

    def slot_step(s, _):
        pl.when(s < groups)(lambda: own_state(s))
        pl.when((s >= delay) & (s < delay + groups))(lambda: prefix(s - delay))
        pl.when(s < ahead)(lambda: w_swap(1 + s // chunks, s % chunks).start())
        pl.when(s == 1)(first_loads)
        pl.when(s == groups)(lambda: w_load(0).start())
        pl.when(s == groups)(score)
        local_turn = (s >= groups) & (s < 2 * groups)
        pl.when(local_turn)(lambda: inside(s - groups, range(1)))
        pl.when(local_turn & (iz == n_z - 1))(lambda: inside(s - groups, range(1, blocks)))
        pl.when((s >= late) & (s < late + groups))(lambda: norm(s - late, range(1)))
        return 0

    lax.fori_loop(0, slots, slot_step, 0)
    for k in range(ahead, (n_y - 1) * chunks):
        w_swap(1 + k // chunks, k % chunks).start()

    def project(rows, r, first, tiles, store):

        def tile(j, _):
            cols = pl.ds(pl.multiple_of(first + j * GROUP, GROUP), GROUP)
            value = jnp.dot(own_n[rows, :], w_own[r, :, cols], preferred_element_type=F32)
            value = value + jnp.dot(sib_n[rows, :], w_sib[r, :, cols], preferred_element_type=F32)
            store(rows, j, cols, value)
            return 0

        lax.fori_loop(0, tiles, tile, 0)

    y_copies = {}

    near = list(range(chunks))

    def send_rows(k, low, high):
        rows = slice(low, high)
        for r in range(1, n_y):
            if k == 0:
                w_load(r).wait()
            for p in range(parts):
                if k == 0:
                    for c in range(p * part // GROUP, (p + 1) * part // GROUP):
                        w_swap(r, c).wait_recv()

                def store(rows, j, cols, value, r=r, p=p):
                    y_send[r - 1, p, rows, span_of(j)] = value.astype(BF16)

                project(rows, r, p * part, part // GROUP, store)
                span = pl.ds(low, high - low)
                at = k * parts + p
                y_copies[k, r, p] = remote(
                    y_send.at[r - 1, p, span], y_recv.at[r - 1, p, span],
                    ys_send.at[r - 1, at], ys_recv.at[r - 1, at],
                    ctx, (iy + r) % n_y * 2 + core,
                )
                y_copies[k, r, p].start()
                if near:
                    w_swap(0, near.pop(0)).start()

    stretches = [(0, BLOCK), (BLOCK, toks)]
    def later_rows(g, _):
        pl.when(iz < n_z - 1)(lambda: inside(g, range(1, blocks)))
        norm(g, range(1, blocks))
        return 0

    for k, (low, high) in enumerate(stretches):
        if k == 1:
            lax.fori_loop(0, groups, later_rows, 0)
        for b in range(low // BLOCK, high // BLOCK):
            for g in range(groups):
                n_copy(g, b).wait_recv()
        send_rows(k, low, high)

    for c in near:
        w_swap(0, c).start()
    w_load(0).wait()
    for c in range(chunks):
        w_swap(0, c).wait_recv()

    def keep(rows, j, cols, value):
        local[rows, cols] = value

    project(slice(0, toks), 0, 0, chunks, keep)

    for k, (low, high) in enumerate(stretches):
        rows = slice(low, high)
        for p in range(parts):
            cols = slice(p * part, (p + 1) * part)
            total = local[rows, cols]
            for r in range(1, n_y):
                y_copies[k, r, p].wait_recv()
                total = total + y_recv[r - 1, p, rows, :].astype(F32)
            out_ref[rows, cols] = total.astype(BF16)

    @pl.when(ctx < n_ctx - 1)
    def _():
        for copy in rims:
            copy.wait_send()

    @pl.when(iz < n_z - 1)
    def _():
        for q in range(width // BLOCK):
            z_copy(q).wait_send()

    for g in range(groups):
        for b in range(blocks):
            n_copy(g, b).wait_send()
    for q in range(width // BLOCK):
        for r in range(1, n_x):
            x_copy(r, q).wait_send()
    for r in range(n_y):
        for c in range(chunks):
            w_swap(r, c).wait_send()
    for copy in y_copies.values():
        copy.wait_send()


def solution(mesh):
    n_ctx, n_tp = mesh.shape["ctx"], mesh.shape["tp"]
    n_x = max(1, n_ctx // 4)

    def body(x_in, bc_in, z_in, codes, head_rate, conv_x, conv_bc, bias_x, bias_bc, skip, norm_gain, w_out):
        toks, width = x_in.shape
        maps = bc_in.shape[1]
        n_state = maps // 2
        depth, model = w_out.shape
        owned = model // n_tp
        part = min(owned, 512)
        n_y = n_tp // 2
        far = max(1, n_y - 1)
        row = max(1, n_x - 1)
        groups = width // GROUP
        strips = width // BLOCK
        blocks = toks // BLOCK
        vmem = pl.BlockSpec(memory_space=pltpu.VMEM)
        hbm = pl.BlockSpec(memory_space=pl.ANY)
        smem = pl.BlockSpec(memory_space=pltpu.SMEM)
        dma = pltpu.SemaphoreType.DMA
        pieces = 2 * (owned // part)
        return pl.pallas_call(
            functools.partial(layer, n_ctx, n_tp, n_x),
            out_shape=pltpu.VMEM((toks, owned), BF16),
            in_specs=[hbm, vmem, hbm, vmem, smem, vmem, vmem, vmem, vmem, smem, vmem, hbm],
            out_specs=vmem,
            scratch_shapes=[
                pltpu.VMEM((toks, width), BF16),
                pltpu.VMEM((toks, width), BF16),
                pltpu.VMEM((toks, toks), BF16),
                pltpu.VMEM((RIM, width), BF16),
                pltpu.VMEM((RIM, maps), BF16),
                pltpu.VMEM((toks, toks), BF16),
                pltpu.VMEM((toks, width), BF16),
                pltpu.VMEM((8, width), F32),
                pltpu.VMEM((8, width), F32),
                pltpu.VMEM((toks, width), F32),
                pltpu.VMEM((toks, maps), BF16),
                pltpu.VMEM((n_state, toks), BF16),
                pltpu.VMEM((toks, width), BF16),
                pltpu.VMEM((toks, width), BF16),
                pltpu.VMEM((n_x, n_state + RIM, width), BF16),
                pltpu.VMEM((n_state, width), BF16),
                pltpu.VMEM((n_state, width), BF16),
                pltpu.VMEM((n_state, width), BF16),
                pltpu.VMEM((toks, width), F32),
                pltpu.VMEM((toks, width), F32),
                pltpu.VMEM((toks, width), BF16),
                pltpu.VMEM((toks, width), BF16),
                pltpu.VMEM((n_y, depth, owned), BF16),
                pltpu.VMEM((n_y, depth, owned), BF16),
                pltpu.VMEM((far, owned // part, toks, part), BF16),
                pltpu.VMEM((far, owned // part, toks, part), BF16),
                pltpu.VMEM((toks, owned), F32),
                dma((groups,)), dma((1,)), dma((2,)), dma((2,)),
                dma((n_y,)), dma((n_y, owned // GROUP)), dma((n_y, owned // GROUP)),
                dma((row, strips)), dma((row, strips)),
                dma((strips,)), dma((strips,)),
                dma((groups, blocks)), dma((groups, blocks)),
                dma((far, pieces)), dma((far, pieces)),
            ],
            compiler_params=pltpu.CompilerParams(
                collective_id=0, has_side_effects=True, vmem_limit_bytes=58 * 1024 * 1024
            ),
        )(x_in, bc_in, z_in, codes.T, head_rate, conv_x, conv_bc, bias_x[None], bias_bc[None], skip,
          norm_gain[None], w_out)

    in_specs = (
        P("ctx", "tp"), P("ctx", None), P("ctx", "tp"), P("ctx", "tp"), P("tp"), P(None, "tp"),
        P(), P("tp"), P(), P("tp"), P("tp"), P("tp", None),
    )
    return jax.shard_map(body, mesh=mesh, in_specs=in_specs, out_specs=P("ctx", "tp"), check_vma=False)
```
